768 devices in a mesh: col: 96 (over x, z, core), node: 8 (over y).
Axes of the slice: x: 4, y: 8, z: 12, core: 2. Of those that a mesh axis runs over, the one named last changes fastest.
Arguments:
- features: bfloat16 [768, 98304], P('col', 'node'), may hold values from -6 to 6
- w_one: bfloat16 [2, 768, 1024], P(None, 'col'), may hold values from -0.15625 to 0.15625
- adj_one: bfloat16 [96, 8, 128, 128], P('node'), may hold values from -0.1875 to 0.1875
- list_one: int32 [96, 8], P('node'), may hold values from 0 to 95
- adj_two: bfloat16 [12288, 4, 128], P(('node', 'col')), may hold values from -0.25 to 0.25
- list_two: int32 [96, 4], P('node'), may hold values from 0 to 11, as said below
- w_two: bfloat16 [2, 1024, 153], replicated, may hold values from -0.1875 to 0.1875
- cotangent: bfloat16 [12288, 153], P(('node', 'col')), may hold values from -6 to 6
Outputs:
- hidden: bfloat16 [12288, 1024], P(('node', 'col'))
- logits: float32 [12288, 153], P(('node', 'col'))
- neighbor_grad: float32 [1024, 153], replicated
The draws below stay inside these ranges and needn't reach their ends.
Inputs may be any that keep to these rules, and one draw needn't show every extreme that they name: `list_two`: each row names 4 different blocks.
All inputs are finite; a program needn't handle non-finite values.
Results may differ from the reference program's by a relative error of at most 0.0054.
Values may be sent and summed in bfloat16 or wider, within the bound.
No kernel may reach another device: no remote copies, remote signals or barrier semaphores. Data moves between devices by JAX's collectives and lax.ppermute only.
A program may use at most 32 MiB of HBM per device.

```python
import jax
import jax.numpy as jnp
from jax import lax

F = 768
HID = 1024
CLS = 153
BLK = 128
H = 1536
HB = 12
SB = 96
SRC = 12288
K1 = 8
K2 = 4
ROWS = 12288
SOURCES = 98304
N_NODE = 8


def draw_list_two(key, part):
    key = jax.random.fold_in(key, 7)
    keys = jax.random.split(key, N_NODE * HB)
    rows = jax.vmap(lambda k: jax.random.permutation(k, HB)[:K2])(keys)
    return rows.astype(jnp.int32)


def set_ends(result, key, smallest, top_value):
    index_at = [jax.random.randint(jax.random.fold_in(key, axis), (), 0, length) for axis, length in enumerate(result.shape)]
    longest = result.shape.index(max(result.shape))
    next_to = index_at[:longest] + [(index_at[longest] + 1) % result.shape[longest]] + index_at[longest + 1:]
    return result.at[tuple(index_at)].set(smallest).at[tuple(next_to)].set(top_value)


def levels(stream_key, extent, cuts, smallest, top_value):
    loudness = 1.0
    for position, blocks in cuts:
        heights = jax.random.uniform(jax.random.fold_in(jax.random.fold_in(stream_key, 6), position), (blocks,), jnp.float32, smallest / len(cuts), top_value / len(cuts))
        loudness = loudness * jnp.repeat(jnp.exp(heights), extent[position] // blocks).reshape((-1,) + (1,) * (len(extent) - 1 - position))
    return loudness


def normal_values(key, shape, spread, limit, cuts=(), held_as=jnp.bfloat16):
    loudness = levels(key, shape, cuts, -0.22, 0.18) if cuts else 1.0
    result = jax.random.normal(key, shape, jnp.float32) * spread * loudness
    return jnp.minimum(jnp.maximum(result, -limit), limit).astype(held_as)


def setup_inputs(seed: int = 0) -> dict:
    streams_of = jax.random.split(jax.random.key(seed), 9)
    return {
        "features": normal_values(streams_of[0], (F, SOURCES), 1.0, 6.0, ((0, 96), (1, 8))),
        "w_one": normal_values(streams_of[1], (2, F, HID), (2 * F) ** -0.5, 0.15625, ((1, 96),)),
        "adj_one": normal_values(streams_of[2], (N_NODE * HB, K1, BLK, BLK), (K1 * BLK) ** -0.5, 0.1875, ((0, 8),)),
        "list_one": set_ends(jax.random.randint(streams_of[3], (N_NODE * HB, K1), 0, SB), jax.random.fold_in(streams_of[3], 1), 0, SB - 1).astype(jnp.int32),
        "adj_two": normal_values(streams_of[4], (ROWS, K2, BLK), (K2 * BLK) ** -0.5, 0.25, ((0, 768),)),
        "list_two": draw_list_two(jax.random.fold_in(streams_of[8], 71), 0),
        "w_two": normal_values(streams_of[6], (2, HID, CLS), HID ** -0.5, 0.1875),
        "cotangent": normal_values(streams_of[7], (ROWS, CLS), 1.0, 6.0, ((0, 768),)),
    }


def reference(features, w_one, adj_one, list_one, adj_two, list_two, w_two, cotangent):
    feature_slices = features.reshape(F, N_NODE, SB, BLK).transpose(1, 0, 2, 3)
    lists_one = list_one.reshape(N_NODE, HB, K1)
    adjs_one = adj_one.reshape(N_NODE, HB, K1, BLK, BLK)
    adjs_two = adj_two.reshape(N_NODE, HB, BLK, K2, BLK)
    second_neighbor_lists = list_two.reshape(N_NODE, HB, K2)
    cots = cotangent.reshape(N_NODE, H, CLS)

    def column_group(packed):
        blocks, lst_one, adj_a, second_adjacency, lst_two, cot = packed
        chosen_nodes = jnp.take(blocks, lst_one, axis=1)
        first_aggregate = jnp.einsum('fhks,hkts->fht', chosen_nodes.astype(jnp.float32), adj_a.astype(jnp.float32))
        first_aggregate = first_aggregate.astype(jnp.bfloat16).reshape(F, H)
        own = blocks.reshape(F, SRC)[:, :H]
        inputs = jnp.stack([first_aggregate, own]).astype(jnp.float32)
        pre = jnp.einsum('ifr,ifh->rh', inputs, w_one.astype(jnp.float32))
        hidden = jnp.maximum(pre, 0.0).astype(jnp.bfloat16)
        neighbor_ids = jnp.take(hidden.reshape(HB, BLK, HID), lst_two, axis=0)
        second_aggregate = jnp.einsum('nlgv,ngvc->nlc', second_adjacency.astype(jnp.float32), neighbor_ids.astype(jnp.float32))
        second_aggregate = second_aggregate.reshape(H, HID).astype(jnp.bfloat16)
        logits = jnp.dot(second_aggregate, w_two[0], preferred_element_type=jnp.float32) + jnp.dot(hidden, w_two[1], preferred_element_type=jnp.float32)
        grad = jnp.dot(second_aggregate.T, cot, preferred_element_type=jnp.float32)
        return hidden, logits, grad

    hiddens, logits, grads = lax.map(column_group, (feature_slices, lists_one, adjs_one, adjs_two, second_neighbor_lists, cots))
    return hiddens.reshape(ROWS, HID), logits.reshape(ROWS, CLS), jnp.sum(grads, axis=0)
```

```python
import jax
import jax.numpy as jnp
from jax import lax
from jax.sharding import Mesh, PartitionSpec as P

F32, BF16 = jnp.float32, jnp.bfloat16


def exchange(parts, axis):
    return lax.all_to_all(parts, axis, 0, 0, tiled=True)


def to_all(part, axis, size):
    return exchange(jnp.broadcast_to(part[None], (size, *part.shape)), axis)


def per_device(features, w_one, adj_one, list_one, adj_two, list_two, w_two, cotangent):
    cols, sources = features.shape
    blocks, fanout = list_one.shape
    block = adj_one.shape[-1]
    mine = adj_two.shape[0]
    lanes = block // mine
    hid = w_one.shape[-1]
    nodes = lax.axis_size("node")
    wide = hid // lanes
    cls = cotangent.shape[-1]
    share = -(-cls // blocks)

    tiles = features.reshape(cols, sources // block, block)
    chosen = jnp.take(tiles, list_one, axis=1)
    agg = jnp.einsum("fhks,hkts->hft", chosen, adj_one, preferred_element_type=F32)
    own = tiles[:, :blocks].transpose(1, 0, 2)
    inputs = jnp.concatenate([agg.astype(BF16), own], axis=1)
    weights = jnp.broadcast_to(w_one.reshape(1, 2 * cols, hid), (blocks, 2 * cols, hid))
    got = exchange(jnp.concatenate([inputs, weights], axis=2), "block")
    got = got.reshape(blocks * 2 * cols, block + hid)
    part = jnp.einsum(
        "kr,kjh->jrh",
        got[:, :block],
        got[:, block:].reshape(-1, lanes, wide),
        preferred_element_type=F32,
    ).astype(BF16)
    edges = adj_two.reshape(mine * adj_two.shape[1], block)
    cot = jnp.pad(cotangent, ((0, 0), (0, 2 * block - cls))).reshape(2 * mine, block)
    extra = jnp.concatenate([edges, cot], axis=0)
    extra = jnp.broadcast_to(extra[None], (lanes, *extra.shape))
    got = exchange(jnp.concatenate([part, extra], axis=1), "lane")
    pre = jnp.sum(got[:, :block].astype(F32), axis=0)
    hidden = jnp.maximum(pre, 0.0).astype(BF16)
    edges = got[:, block : block + edges.shape[0]].reshape(block, -1, block)
    cot = got[:, block + edges.shape[1] * mine :].reshape(block, 2 * block)

    every = to_all(hidden, "block", blocks)
    listed = lax.dynamic_index_in_dim(list_two, lax.axis_index("block"), 0, keepdims=False)
    near = jnp.take(every, listed, axis=0)
    second = jnp.einsum("rks,ksh->rh", edges, near, preferred_element_type=F32).astype(BF16)
    grad = jnp.einsum("rc,rh->ch", cot, second, preferred_element_type=F32)
    grad = grad[: blocks * share].reshape(blocks, share, wide).astype(BF16)
    grad = jnp.sum(exchange(grad, "block").astype(F32), axis=0)
    grad = jnp.sum(to_all(grad, "node", nodes), axis=0).astype(BF16)
    grad = to_all(grad, "block", blocks).reshape(blocks * share, wide)

    rows = jnp.stack([second, hidden]).reshape(2, lanes, mine, wide)
    rows = rows.transpose(1, 0, 2, 3).reshape(lanes, 2 * mine, wide)
    grad = jnp.broadcast_to(grad[None], (lanes, *grad.shape))
    got = exchange(jnp.concatenate([rows, grad], axis=1), "lane")
    both = got[:, : 2 * mine].reshape(lanes, 2, mine, wide).transpose(2, 1, 0, 3)
    both = both.reshape(mine, 2, hid)
    logits = jnp.einsum("rih,ihc->rc", both, w_two, preferred_element_type=F32)
    grad = got[:, 2 * mine : 2 * mine + cls].transpose(0, 2, 1).reshape(hid, cls).astype(F32)
    return both[:, 1], logits, grad


def solution(mesh):
    cols, nodes = mesh.devices.shape
    lanes = 8
    fine = Mesh(mesh.devices.reshape(cols // lanes, lanes, nodes), ("block", "lane", "node"))
    col = ("block", "lane")
    rows = ("node", "block", "lane")
    in_specs = (
        P(col, "node"),
        P(None, col, None),
        P("node", None, None, None),
        P("node", None),
        P(rows, None, None),
        P("node", None),
        P(),
        P(rows, None),
    )
    out_specs = (P(rows, None), P(rows, None), P())
    return jax.shard_map(
        per_device, mesh=fine, in_specs=in_specs, out_specs=out_specs, check_vma=False
    )
```

```python
import jax
import jax.numpy as jnp
from jax import lax
from jax.sharding import Mesh, PartitionSpec as P

F32, BF16 = jnp.float32, jnp.bfloat16
LANE = ("x", "c")


def exchange(parts, axis):
    return lax.all_to_all(parts, axis, 0, 0, tiled=True)


def to_all(part, axis, size):
    return exchange(jnp.broadcast_to(part[None], (size, *part.shape)), axis)


def per_device(features, w_one, adj_one, list_one, adj_two, list_two, w_two, cotangent):
    cols, sources = features.shape
    blocks, fanout = list_one.shape
    block = adj_one.shape[-1]
    mine = adj_two.shape[0]
    lanes = block // mine
    hid = w_one.shape[-1]
    nodes = lax.axis_size("node")
    wide = hid // lanes
    cls = cotangent.shape[-1]
    share = -(-cls // blocks)
    xs = lax.axis_size("x")
    strips = block // (mine * lax.axis_size("c"))
    mid, low = lax.axis_index("z") // strips, lax.axis_index("z") % strips

    tiles = features.reshape(cols, sources // block, block)
    chosen = tiles.at[:, list_one].get(mode="promise_in_bounds")
    agg = jnp.einsum("fhks,hkts->hft", chosen, adj_one, preferred_element_type=F32)
    own = tiles[:, :blocks].transpose(1, 0, 2)
    inputs = jnp.concatenate([agg.astype(BF16), own], axis=1)
    weights = jnp.broadcast_to(w_one.reshape(1, 2 * cols, hid), (blocks, 2 * cols, hid))
    got = exchange(jnp.concatenate([inputs, weights], axis=2), "z")
    got = got.reshape(blocks * 2 * cols, block + hid)
    part = jnp.einsum(
        "kr,kjh->jrh",
        got[:, :block],
        got[:, block:].reshape(-1, lanes, wide),
        preferred_element_type=F32,
    ).astype(BF16)
    edges = adj_two.reshape(mine * adj_two.shape[1], block)
    cot = jnp.pad(cotangent, ((0, 0), (0, 2 * block - cls))).reshape(2 * mine, block)
    extra = jnp.concatenate([edges, cot], axis=0)
    extra = jnp.broadcast_to(extra[None], (lanes, *extra.shape))
    got = exchange(jnp.concatenate([part, extra], axis=1), LANE)
    pre = jnp.sum(got[:, :block].astype(F32), axis=0)
    hidden = jnp.maximum(pre, 0.0).astype(BF16)
    edges = got[:, block : block + edges.shape[0]].reshape(xs, block // xs, -1, block)
    cot = got[:, block + mine * edges.shape[2] :].reshape(block, 2 * block)

    every = to_all(hidden, "z", blocks)
    lists = list_two.reshape(xs, blocks // xs, -1)
    lists = lax.dynamic_index_in_dim(lists, mid, 1, keepdims=False)
    near = every.at[lists].get(mode="promise_in_bounds")
    second = jnp.einsum("xrks,xksh->xrh", edges, near, preferred_element_type=F32)
    second = second.astype(BF16).reshape(block, wide)
    held = every.reshape(xs, blocks // xs, strips, block // xs, wide)
    held = lax.dynamic_slice(held, (0, mid, low, 0, 0), (xs, 1, 1, block // xs, wide))
    grad = jnp.einsum("rc,rh->ch", cot, second, preferred_element_type=F32)
    grad = grad[: blocks * share].reshape(blocks, share, wide).astype(BF16)
    grad = jnp.sum(exchange(grad, "z").astype(F32), axis=0)
    grad = jnp.sum(to_all(grad, "node", nodes), axis=0).astype(BF16)
    grad = to_all(grad, "z", blocks).reshape(blocks * share, wide)

    rows = [second.reshape(lanes, mine, wide), held.reshape(lanes, mine, wide)]
    grad = jnp.broadcast_to(grad[None], (lanes, *grad.shape))
    got = exchange(jnp.concatenate([*rows, grad], axis=1), LANE)
    both = got[:, : 2 * mine].reshape(lanes, 2, mine, wide).transpose(2, 1, 0, 3)
    both = both.reshape(mine, 2, hid)
    logits = jnp.einsum("rih,ihc->rc", both, w_two, preferred_element_type=F32)
    grad = got[:, 2 * mine : 2 * mine + cls].transpose(0, 2, 1).reshape(hid, cls).astype(F32)
    return both[:, 1], logits, grad


def solution(mesh):
    nodes = mesh.devices.shape[1]
    fine = Mesh(mesh.devices.reshape(4, 12, 2, nodes), ("x", "z", "c", "node"))
    col = ("x", "z", "c")
    rows = ("node", *col)
    in_specs = (
        P(col, "node"),
        P(None, col, None),
        P("node", None, None, None),
        P("node", None),
        P(rows, None, None),
        P("node", None),
        P(),
        P(rows, None),
    )
    out_specs = (P(rows, None), P(rows, None), P())
    return jax.shard_map(
        per_device, mesh=fine, in_specs=in_specs, out_specs=out_specs, check_vma=False
    )
```

```python
import jax
import jax.numpy as jnp
from jax import lax
from jax.sharding import Mesh, PartitionSpec as P

F32, BF16 = jnp.float32, jnp.bfloat16
LANE = ("x", "c")


def exchange(parts, axis):
    return lax.all_to_all(parts, axis, 0, 0, tiled=True)


def to_all(part, size):
    return jnp.broadcast_to(part[None], (size, *part.shape))


def dot(spec, a, b):
    return jnp.einsum(spec, a, b, preferred_element_type=F32)


def two(a):
    high = a.astype(BF16)
    return high, (a - high.astype(F32)).astype(BF16)


def per_device(features, w_one, adj_one, list_one, adj_two, list_two, w_two, cotangent):
    cols, sources = features.shape
    blocks, fanout = list_one.shape
    block = adj_one.shape[-1]
    mine, listed = adj_two.shape[:2]
    hid, cls = w_two.shape[1:]
    xs, cores = lax.axis_size("x"), lax.axis_size("c")
    lanes = xs * cores
    wide = hid // lanes
    by_lane = -(-cls // (8 * lanes)) * 8
    every = by_lane * lanes
    by_z = every // blocks
    kept = -(-cls // 8) * 8
    strip = mine * cores
    strips = block // strip
    mids = blocks // xs
    place = lax.axis_index("z")
    lane = lax.axis_index("x") * cores + lax.axis_index("c")
    lists = list_two.reshape(xs, mids, listed)
    lists = lax.dynamic_index_in_dim(lists, place // strips, 1, keepdims=False)

    shape = (xs, block, strips, block)
    x_of, row, low_of, to = (lax.broadcasted_iota(jnp.int32, shape, i) for i in range(4))
    move = (row // strip == low_of) & (to // strip == x_of) & (row % strip == to % strip)
    move = move.astype(BF16)

    def to_z(a):
        a = a.reshape(xs, mids, -1, block)
        return dot("xmkl,xlzr->mzkr", a, move).astype(BF16).reshape(blocks, -1, block)

    def to_blocks(a):
        a = a.reshape(mids, strips, -1, block)
        return dot("mzkr,xlzr->xmkl", a, move).astype(BF16).reshape(blocks, -1, block)

    edges = to_all(adj_two.reshape(mine * listed, block), lanes)
    cot = jnp.pad(cotangent, ((0, 0), (0, every - cls))).reshape(mine, lanes, by_lane)
    cot = jnp.pad(cot.transpose(1, 0, 2), ((0, 0), (0, 0), (0, block - by_lane)))
    got = exchange(jnp.concatenate([edges, cot], axis=1), LANE)
    edges = got[:, : mine * listed].reshape(xs, strip, listed, block)
    cot = got[:, mine * listed :, :by_lane].reshape(xs, strip, by_lane)

    tiles = features.reshape(cols, sources // block, block)
    chosen = tiles.at[:, list_one].get(mode="promise_in_bounds")
    agg = dot("fhks,hkts->hft", chosen, adj_one).astype(BF16)
    own = tiles[:, :blocks].transpose(1, 0, 2)
    inputs = to_z(jnp.concatenate([agg, own], axis=1))
    weights = w_one.reshape(2 * cols, lanes, wide).transpose(1, 0, 2).reshape(-1, wide)
    back = dot("xrc,xrks->xkcs", cot, edges)
    hits = lists[:, :, None] == jnp.arange(blocks, dtype=jnp.int32)
    back = jnp.where(hits[..., None, None], back[:, :, None], 0.0).sum((0, 1)).astype(BF16)
    got = [inputs, to_z(back), to_all(weights, blocks)]
    got = exchange(jnp.concatenate(got, axis=1), "z")
    inputs, back, weights = jnp.split(got, (2 * cols, 2 * cols + by_lane), axis=1)
    weights = weights.reshape(blocks, lanes, 2 * cols, wide)
    part = dot("zkr,zjkh->jrh", inputs, weights).astype(BF16)
    back = jnp.concatenate(two(jnp.sum(back.astype(F32), axis=0)), axis=0)

    got = exchange(jnp.concatenate([part, to_all(back, lanes)], axis=1), LANE)
    pre = jnp.sum(got[:, :block].astype(F32), axis=0)
    hidden = jnp.maximum(pre, 0.0).astype(BF16)
    high = got[:, block : block + by_lane].reshape(every, block)
    low = got[:, block + by_lane :].reshape(every, block)
    grad = dot("cr,rh->ch", high, hidden) + dot("cr,rh->ch", low, hidden)
    grad = jnp.sum(exchange(grad.reshape(blocks, by_z, wide), "z"), axis=0)
    grad = lax.psum(grad, "node").astype(BF16)

    near_w = lax.dynamic_slice(w_two, (0, lane * wide, 0), (1, wide, cls))[0]
    near_w = jnp.pad(near_w, ((0, 0), (0, every - cls)))
    product = dot("hc,rh->cr", near_w, hidden).astype(BF16).reshape(lanes, by_lane, block)
    rows = hidden.reshape(lanes, mine, wide)
    got = exchange(jnp.concatenate([product, rows], axis=1), LANE)
    product = jnp.sum(got[:, :by_lane].astype(F32), axis=0).astype(BF16)
    hidden = got[:, by_lane:].transpose(1, 0, 2).reshape(mine, hid)
    own_logits = dot("rh,hc->rc", hidden, w_two[1])

    got = exchange(to_all(jnp.concatenate([grad, product], axis=0), blocks), "z")
    grad = got[:, :by_z].reshape(every, wide)[:kept]
    near = to_blocks(got[:, by_z:]).at[lists].get(mode="promise_in_bounds")
    logits = dot("xrks,xkcs->xrc", edges, near).reshape(lanes, mine, by_lane)
    logits = jnp.concatenate(two(logits), axis=2)
    logits = jnp.pad(logits, ((0, 0), (0, 0), (0, wide - 2 * by_lane)))
    got = exchange(jnp.concatenate([to_all(grad, lanes), logits], axis=1), LANE)
    logits = got[:, kept:].astype(F32)
    logits = logits[..., :by_lane] + logits[..., by_lane : 2 * by_lane]
    logits = logits.transpose(1, 0, 2).reshape(mine, every)[:, :cls] + own_logits
    grad = got[:, :cls].transpose(0, 2, 1).reshape(hid, cls).astype(F32)
    return hidden, logits, grad


def solution(mesh):
    nodes = mesh.devices.shape[1]
    fine = Mesh(mesh.devices.reshape(4, 12, 2, nodes), ("x", "z", "c", "node"))
    col = ("x", "z", "c")
    rows = ("node", *col)
    in_specs = (
        P(col, "node"),
        P(None, col, None),
        P("node", None, None, None),
        P("node", None),
        P(rows, None, None),
        P("node", None),
        P(),
        P(rows, None),
    )
    out_specs = (P(rows, None), P(rows, None), P())
    return jax.shard_map(
        per_device, mesh=fine, in_specs=in_specs, out_specs=out_specs, check_vma=False
    )
```

```python
import jax
import jax.numpy as jnp
import numpy as np
from jax import lax
from jax.sharding import Mesh, PartitionSpec as P

F32, BF16 = jnp.float32, jnp.bfloat16
LANE = ("x", "c")


def exchange(parts, axis):
    return lax.all_to_all(parts, axis, 0, 0, tiled=True)


def to_all(part, size):
    return jnp.broadcast_to(part[None], (size, *part.shape))


def dot(spec, a, b):
    return jnp.einsum(spec, a, b, preferred_element_type=F32)


def two(a):
    high = a.astype(BF16)
    return jnp.concatenate([high, (a - high.astype(F32)).astype(BF16)], axis=-2)


def per_device(features, w_one, adj_one, list_one, adj_two, list_two, w_two, cotangent):
    cols, sources = features.shape
    blocks, fanout = list_one.shape
    block = adj_one.shape[-1]
    mine, listed = adj_two.shape[:2]
    hid, cls = w_two.shape[1:]
    nodes = lax.axis_size("node")
    xs, cores = lax.axis_size("x"), lax.axis_size("c")
    lanes = xs * cores
    wide = hid // lanes
    by_lane = -(-cls // (8 * lanes)) * 8
    every = by_lane * lanes
    by_z = every // blocks
    kept = -(-cls // 8) * 8
    strip = mine * cores
    strips = block // strip
    mids = blocks // xs
    place, my_x, my_c = (lax.axis_index(axis) for axis in ("z", "x", "c"))
    lists = list_two.reshape(xs, mids, listed)
    lists = lax.dynamic_index_in_dim(lists, place // strips, 1, keepdims=False)

    edges = adj_two.reshape(mine * listed, block)
    cot = jnp.pad(cotangent, ((0, 0), (0, every - by_lane + block - cls)))
    cot = [lax.slice_in_dim(cot, j * by_lane, j * by_lane + block, axis=1) for j in range(lanes)]
    got = exchange(jnp.stack([jnp.concatenate([edges, c], axis=0) for c in cot]), LANE)
    edges = got[:, : mine * listed].reshape(xs, strip, listed, block)
    cot = got[:, mine * listed :].reshape(xs, strip, block)

    tiles = features.reshape(cols, sources // block, block)
    ids = jnp.concatenate([list_one.reshape(-1).astype(jnp.uint32), jnp.arange(blocks, dtype=jnp.uint32)])
    chosen = tiles.at[:, ids].get(mode="promise_in_bounds")
    own = chosen[:, blocks * fanout :].transpose(1, 0, 2)
    chosen = chosen[:, : blocks * fanout].reshape(cols, blocks, fanout, block)
    agg = dot("fhks,hkts->hft", chosen, adj_one).astype(BF16)
    back = dot("xrc,xrks->xkcs", cot, edges)[:, :, :by_lane]
    hits = lists[:, :, None] == jnp.arange(blocks, dtype=jnp.int32)
    back = jnp.where(hits[..., None, None], back[:, :, None], 0.0).sum((0, 1)).astype(BF16)
    at = np.arange(block)
    move = np.zeros((xs, block, strips, block), np.float32)
    for x in range(xs):
        for low in range(strips):
            move[x, :, low] = at[:, None] - low * strip == at - x * strip
            move[x, :, low, : x * strip] = move[x, :, low, (x + 1) * strip :] = 0
    sends = jnp.concatenate([agg, own, back], axis=1).reshape(xs, mids, -1, block)
    sends = dot("xmkl,xlzr->mzkr", sends, jnp.asarray(move, BF16)).astype(BF16)
    sends = sends.reshape(blocks, -1, block)
    weights = w_one.reshape(2, cols, lanes, wide).transpose(0, 2, 1, 3).reshape(-1, wide)
    got = exchange(jnp.concatenate([sends, to_all(weights, blocks)], axis=1), "z")
    inputs, back, weights = jnp.split(got, (2 * cols, 2 * cols + by_lane), axis=1)
    inputs = inputs.reshape(blocks, 2, cols, block)
    weights = weights.reshape(blocks, 2, lanes, cols, wide)
    part = dot("zikr,zijkh->jrh", inputs, weights).astype(BF16)
    back = two(jnp.sum(back.astype(F32), axis=0))

    rows = part.reshape(lanes, lanes, mine, wide).transpose(1, 0, 2, 3)
    rows = rows.reshape(lanes, lanes * mine, wide)
    got = exchange(jnp.concatenate([part, rows, to_all(back, lanes)], axis=1), LANE)
    hidden = jnp.maximum(jnp.sum(got[:, : 2 * block].astype(F32), axis=0), 0.0).astype(BF16)
    rows = hidden[block:].reshape(lanes, mine, wide).transpose(1, 0, 2).reshape(mine, hid)
    hidden = hidden[:block]
    back = got[:, 2 * block :].reshape(lanes, 2, by_lane, block)
    grad = dot("jcr,rh->jch", back[:, 0], hidden) + dot("jcr,rh->jch", back[:, 1], hidden)
    both = dot("rh,ihc->irc", rows, w_two)
    product = jnp.pad(both[0].astype(BF16), ((0, 0), (0, 2 * block - cls)))
    product = jnp.concatenate([product[:, :block], product[:, block:]], axis=0)
    grad = two(grad.reshape(blocks, by_z, wide))
    got = exchange(jnp.concatenate([grad, to_all(product, blocks)], axis=1), "z")
    grad = jnp.sum(got[:, : 2 * by_z].astype(F32), axis=0)
    grad = grad[:by_z] + grad[by_z:]
    grad = jnp.sum(exchange(to_all(grad, nodes), "node"), axis=0).astype(BF16)

    hits = lists[:, :, None] == my_x * mids + jnp.arange(mids, dtype=jnp.int32)
    hits = hits.transpose(0, 2, 1)[:, None, :, :, None]
    near = jnp.where(hits, edges[:, :, None], 0).sum(3).reshape(block, mids * block)
    product = got[:, 2 * by_z :].reshape(mids, strips, 2, 1, mine, block).transpose(0, 1, 3, 4, 2, 5)
    held = my_c == jnp.arange(cores).reshape(1, 1, cores, 1, 1, 1)
    product = jnp.where(held, product, 0).reshape(mids * block, 2 * block)
    logits = dot("rs,sc->rc", near, product).astype(BF16).reshape(lanes, mine, 2 * block)
    logits = [logits[..., :block], logits[..., block:]]

    grad = exchange(to_all(grad, blocks), "z").reshape(every, wide)[:kept]
    got = exchange(jnp.concatenate([to_all(grad, lanes), *logits], axis=1), LANE)
    logits = jnp.sum(got[:, kept:].astype(F32), axis=0)
    logits = jnp.concatenate([logits[:mine], logits[mine:]], axis=1)[:, :cls] + both[1]
    grad = got[:, :cls].transpose(0, 2, 1).reshape(hid, cls).astype(F32)
    return rows, logits, grad


def solution(mesh):
    nodes = mesh.devices.shape[1]
    fine = Mesh(mesh.devices.reshape(4, 12, 2, nodes), ("x", "z", "c", "node"))
    col = ("x", "z", "c")
    rows = ("node", *col)
    in_specs = (
        P(col, "node"),
        P(None, col, None),
        P("node", None, None, None),
        P("node", None),
        P(rows, None, None),
        P("node", None),
        P(),
        P(rows, None),
    )
    out_specs = (P(rows, None), P(rows, None), P())
    return jax.shard_map(
        per_device, mesh=fine, in_specs=in_specs, out_specs=out_specs, check_vma=False
    )
```

```python
import jax
import jax.numpy as jnp
import numpy as np
from jax import lax
from jax.sharding import Mesh, PartitionSpec as P

F32, BF16 = jnp.float32, jnp.bfloat16
LANE = ("x", "c")


def exchange(parts, axis):
    return lax.all_to_all(parts, axis, 0, 0, tiled=True)


def to_all(part, size):
    return jnp.broadcast_to(part[None], (size, *part.shape))


def dot(spec, a, b):
    return jnp.einsum(spec, a, b, preferred_element_type=F32)


def two(a):
    high = a.astype(BF16)
    return jnp.concatenate([high, (a - high.astype(F32)).astype(BF16)], axis=-2)


def per_device(features, w_one, adj_one, list_one, adj_two, list_two, w_two, cotangent):
    cols, sources = features.shape
    blocks, fanout = list_one.shape
    block = adj_one.shape[-1]
    mine, listed = adj_two.shape[:2]
    hid, cls = w_two.shape[1:]
    nodes = lax.axis_size("node")
    xs, cores = lax.axis_size("x"), lax.axis_size("c")
    lanes = xs * cores
    wide = hid // lanes
    by_lane = -(-cls // (8 * lanes)) * 8
    every = by_lane * lanes
    by_z = every // blocks
    kept = -(-cls // 8) * 8
    strip = mine * cores
    strips = block // strip
    mids = blocks // xs
    place, my_x, my_c = (lax.axis_index(axis) for axis in ("z", "x", "c"))
    my_lane = my_x * cores + my_c
    mine_of = jnp.arange(blocks) == mids * jnp.arange(xs)[:, None] + place // strips
    lists = dot("xb,bk->xk", mine_of.astype(BF16), list_two.astype(BF16)).astype(jnp.int32)

    edges = adj_two.reshape(mine * listed, block)
    cot = jnp.pad(cotangent, ((0, 0), (0, 2 * block - cls)))
    sends = jnp.concatenate([edges, cot[:, :block], cot[:, block:]], axis=0)
    got = exchange(to_all(sends, lanes), LANE)
    edges = got[:, : mine * listed].reshape(xs, strip, listed, block)
    cot = got[:, mine * listed :].reshape(xs, cores, 2, mine, block)
    pick = jnp.arange(2 * block)[:, None] == my_lane * by_lane + jnp.arange(by_lane)
    pick = pick.reshape(2, block, by_lane).astype(BF16)
    cot = dot("xchit,hts->xcis", cot, pick).astype(BF16).reshape(xs, strip, by_lane)

    tiles = features.reshape(cols, sources // block, block)
    chosen = lax.gather(
        tiles,
        list_one.reshape(-1, 1),
        lax.GatherDimensionNumbers((0, 2), (1,), (1,)),
        (cols, 1, block),
        mode="promise_in_bounds",
    )
    chosen = chosen.reshape(cols, blocks, fanout, block)
    own = tiles[:, :blocks].transpose(1, 0, 2)
    agg = dot("fhks,hkts->hft", chosen, adj_one).astype(BF16)
    back = dot("xrc,xrks->xkcs", cot, edges)
    hits = lists[:, :, None] == jnp.arange(blocks, dtype=jnp.int32)
    back = jnp.where(hits[..., None, None], back[:, :, None], 0.0).sum((0, 1)).astype(BF16)
    at = np.arange(block)
    move = np.zeros((xs, block, strips, block), np.float32)
    for x in range(xs):
        for low in range(strips):
            move[x, :, low] = at[:, None] - low * strip == at - x * strip
            move[x, :, low, : x * strip] = move[x, :, low, (x + 1) * strip :] = 0
    sends = jnp.concatenate([agg, own, back], axis=1).reshape(xs, mids, -1, block)
    sends = dot("xmkl,xlzr->mzkr", sends, jnp.asarray(move, BF16)).astype(BF16)
    sends = sends.reshape(blocks, -1, block)
    weights = w_one.reshape(2, cols, lanes, wide).transpose(0, 2, 1, 3).reshape(-1, wide)
    got = exchange(jnp.concatenate([sends, to_all(weights, blocks)], axis=1), "z")
    inputs, back, weights = jnp.split(got, (2 * cols, 2 * cols + by_lane), axis=1)
    inputs = inputs.reshape(blocks, 2, cols, block)
    weights = weights.reshape(blocks, 2, lanes, cols, wide)
    part = dot("zikr,zijkh->jrh", inputs, weights).astype(BF16)
    back = two(jnp.sum(back.astype(F32), axis=0))

    rows = part.reshape(lanes, lanes, mine, wide).transpose(1, 0, 2, 3)
    rows = rows.reshape(lanes, lanes * mine, wide)
    got = exchange(jnp.concatenate([part, rows, to_all(back, lanes)], axis=1), LANE)
    hidden = jnp.maximum(jnp.sum(got[:, : 2 * block].astype(F32), axis=0), 0.0).astype(BF16)
    rows = hidden[block:].reshape(lanes, mine, wide).transpose(1, 0, 2).reshape(mine, hid)
    hidden = hidden[:block]
    back = got[:, 2 * block :].reshape(lanes, 2, by_lane, block)
    grad = dot("jcr,rh->jch", back[:, 0], hidden) + dot("jcr,rh->jch", back[:, 1], hidden)
    both = dot("rh,ihc->irc", rows, w_two)
    product = jnp.pad(both[0].astype(BF16), ((0, 0), (0, 2 * block - cls)))
    product = jnp.concatenate([product[:, :block], product[:, block:]], axis=0)
    grad = two(grad.reshape(blocks, by_z, wide))
    got = exchange(jnp.concatenate([grad, to_all(product, blocks)], axis=1), "z")
    grad = jnp.sum(got[:, : 2 * by_z].astype(F32), axis=0)
    grad = grad[:by_z] + grad[by_z:]
    grad = jnp.sum(exchange(to_all(grad, nodes), "node"), axis=0).astype(BF16)

    hits = lists[:, :, None] == my_x * mids + jnp.arange(mids, dtype=jnp.int32)
    hits = hits.transpose(0, 2, 1)[:, None, :, :, None]
    near = jnp.where(hits, edges[:, :, None], 0).sum(3).reshape(block, mids * block)
    product = got[:, 2 * by_z :].reshape(mids, strips, 2, 1, mine, block).transpose(0, 1, 3, 4, 2, 5)
    held = my_c == jnp.arange(cores).reshape(1, 1, cores, 1, 1, 1)
    product = jnp.where(held, product, 0).reshape(mids * block, 2 * block)
    logits = dot("rs,sc->rc", near, product).reshape(lanes, mine, 2 * block)
    logits = jnp.concatenate([logits[..., :block], logits[..., block:]], axis=1)

    grad = exchange(to_all(grad, blocks), "z").reshape(every, wide)[:kept]
    got = exchange(jnp.concatenate([to_all(grad, lanes), two(logits)], axis=1), LANE)
    logits = jnp.sum(got[:, kept:].astype(F32), axis=0)
    logits = logits[: 2 * mine] + logits[2 * mine :]
    logits = jnp.concatenate([logits[:mine], logits[mine:]], axis=1)[:, :cls] + both[1]
    grad = got[:, :cls].transpose(0, 2, 1).reshape(hid, cls).astype(F32)
    return rows, logits, grad


def solution(mesh):
    nodes = mesh.devices.shape[1]
    fine = Mesh(mesh.devices.reshape(4, 12, 2, nodes), ("x", "z", "c", "node"))
    col = ("x", "z", "c")
    rows = ("node", *col)
    in_specs = (
        P(col, "node"),
        P(None, col, None),
        P("node", None, None, None),
        P("node", None),
        P(rows, None, None),
        P("node", None),
        P(),
        P(rows, None),
    )
    out_specs = (P(rows, None), P(rows, None), P())
    return jax.shard_map(
        per_device, mesh=fine, in_specs=in_specs, out_specs=out_specs, check_vma=False
    )
```

```python
import jax
import jax.numpy as jnp
import numpy as np
from jax import lax
from jax.experimental import pallas as pl
from jax.experimental.pallas import tpu as pltpu
from jax.sharding import Mesh, PartitionSpec as P

F32, BF16 = jnp.float32, jnp.bfloat16
LANE = ("x", "c")


def exchange(parts, axis):
    return lax.all_to_all(parts, axis, 0, 0, tiled=True)


def to_all(part, size):
    return jnp.broadcast_to(part[None], (size, *part.shape))


def dot(spec, a, b):
    return jnp.einsum(spec, a, b, preferred_element_type=F32)


def two(a):
    high = a.astype(BF16)
    return jnp.concatenate([high, (a - high.astype(F32)).astype(BF16)], axis=-2)


def middle(got, w, sends, rows, logits):
    lanes, wide = got.shape[0], got.shape[2]
    blocks, by_z = sends.shape[0], sends.shape[1] // 4
    block, mine = got.shape[2], rows.shape[0]
    pre = got[0, : 2 * block].astype(F32)
    for j in range(1, lanes):
        pre = pre + got[j, : 2 * block].astype(F32)
    hidden = jnp.maximum(pre, 0.0).astype(BF16)
    for j in range(lanes):
        rows[:, j * wide : (j + 1) * wide] = hidden[block + j * mine : block + (j + 1) * mine]
    hidden = hidden[:block]
    back = got[:, 2 * block :].astype(F32)
    half = back.shape[1] // 2
    back = (back[:, :half] + back[:, half:]).reshape(lanes * half, block)
    high = back.astype(BF16)
    low = (back - high.astype(F32)).astype(BF16)
    grad = jnp.dot(high, hidden, preferred_element_type=F32)
    grad = grad + jnp.dot(low, hidden, preferred_element_type=F32)
    grad = grad.reshape(blocks, by_z, wide)
    high = grad.astype(BF16)
    sends[:, :by_z] = high
    sends[:, by_z : 2 * by_z] = (grad - high.astype(F32)).astype(BF16)
    over = (((1,), (1,)), ((), ()))
    product = lax.dot_general(rows[...], w[0], over, preferred_element_type=F32).astype(BF16)
    logits[...] = lax.dot_general(rows[...], w[1], over, preferred_element_type=F32)
    for z in range(blocks):
        sends[z, 2 * by_z : 2 * by_z + mine] = product[:, :block]
        sends[z, 2 * by_z + mine :] = product[:, block:]


def finish(got, own, logits, grad):
    lanes, wide = got.shape[0], got.shape[2]
    mine, cls = logits.shape
    kept = got.shape[1] - 2 * mine
    part = got[0, kept:].astype(F32)
    for j in range(1, lanes):
        part = part + got[j, kept:].astype(F32)
    part = jnp.concatenate([part[:mine], part[mine:]], axis=1) + own[...]
    logits[...] = part[:, :cls]
    for j in range(lanes):
        grad[:, j * wide : (j + 1) * wide] = got[j, :kept].astype(F32)[:cls]


def per_device(features, w_one, adj_one, list_one, adj_two, list_two, w_two, cotangent):
    cols, sources = features.shape
    blocks, fanout = list_one.shape
    block = adj_one.shape[-1]
    mine, listed = adj_two.shape[:2]
    hid, cls = w_two.shape[1:]
    nodes = lax.axis_size("node")
    xs, cores = lax.axis_size("x"), lax.axis_size("c")
    lanes = xs * cores
    wide = hid // lanes
    by_lane = -(-cls // (8 * lanes)) * 8
    every = by_lane * lanes
    by_z = every // blocks
    kept = -(-cls // 8) * 8
    strip = mine * cores
    strips = block // strip
    mids = blocks // xs
    place, my_x, my_c = (lax.axis_index(axis) for axis in ("z", "x", "c"))
    my_lane = my_x * cores + my_c
    mine_of = jnp.arange(blocks) == mids * jnp.arange(xs)[:, None] + place // strips
    lists = dot("xb,bk->xk", mine_of.astype(BF16), list_two.astype(BF16)).astype(jnp.int32)

    edges = adj_two.reshape(mine * listed, block)
    cot = jnp.pad(cotangent, ((0, 0), (0, 2 * block - cls)))
    sends = jnp.concatenate([edges, cot[:, :block], cot[:, block:]], axis=0)
    got = exchange(to_all(sends, lanes), LANE)
    edges = got[:, : mine * listed].reshape(xs, strip, listed, block)
    cot = got[:, mine * listed :].reshape(xs, cores, 2, mine, block)
    pick = jnp.arange(2 * block)[:, None] == my_lane * by_lane + jnp.arange(by_lane)
    pick = pick.reshape(2, block, by_lane).astype(BF16)
    cot = dot("xchit,hts->xcis", cot, pick).astype(BF16).reshape(xs, strip, by_lane)

    tiles = features.reshape(cols, sources // block, block)
    chosen = lax.gather(
        tiles,
        list_one.reshape(-1, 1),
        lax.GatherDimensionNumbers((0, 2), (1,), (1,)),
        (cols, 1, block),
        mode="promise_in_bounds",
    )
    chosen = chosen.reshape(cols, blocks, fanout, block)
    own = tiles[:, :blocks].transpose(1, 0, 2)
    agg = dot("fhks,hkts->hft", chosen, adj_one).astype(BF16)
    back = dot("xrc,xrks->xkcs", cot, edges)
    hits = lists[:, :, None] == jnp.arange(blocks, dtype=jnp.int32)
    back = jnp.where(hits[..., None, None], back[:, :, None], 0.0).sum((0, 1)).astype(BF16)
    at = np.arange(block)
    move = np.zeros((xs, block, strips, block), np.float32)
    for x in range(xs):
        for low in range(strips):
            move[x, :, low] = at[:, None] - low * strip == at - x * strip
            move[x, :, low, : x * strip] = move[x, :, low, (x + 1) * strip :] = 0
    sends = jnp.concatenate([agg, own, back], axis=1).reshape(xs, mids, -1, block)
    sends = dot("xmkl,xlzr->mzkr", sends, jnp.asarray(move, BF16)).astype(BF16)
    sends = sends.reshape(blocks, -1, block)
    weights = w_one.reshape(2, cols, lanes, wide).transpose(0, 2, 1, 3).reshape(-1, wide)
    got = exchange(jnp.concatenate([sends, to_all(weights, blocks)], axis=1), "z")
    inputs, back, weights = jnp.split(got, (2 * cols, 2 * cols + by_lane), axis=1)
    inputs = inputs.reshape(blocks, 2, cols, block)
    weights = weights.reshape(blocks, 2, lanes, cols, wide)
    part = dot("zikr,zijkh->jrh", inputs, weights).astype(BF16)
    back = two(jnp.sum(back.astype(F32), axis=0))

    rows = part.reshape(lanes, lanes, mine, wide).transpose(1, 0, 2, 3)
    rows = rows.reshape(lanes, lanes * mine, wide)
    got = exchange(jnp.concatenate([part, rows, to_all(back, lanes)], axis=1), LANE)
    w = jnp.pad(w_two.transpose(0, 2, 1), ((0, 0), (0, 2 * block - cls), (0, 0)))
    sends, rows, own_logits = pl.pallas_call(
        middle,
        out_shape=(
            jax.ShapeDtypeStruct((blocks, 4 * by_z, block), BF16),
            jax.ShapeDtypeStruct((mine, hid), BF16),
            jax.ShapeDtypeStruct((mine, 2 * block), F32),
        ),
        compiler_params=pltpu.CompilerParams(vmem_limit_bytes=16 * 2**20),
    )(got, w)
    got = exchange(sends, "z")
    grad = jnp.sum(got[:, : 2 * by_z].astype(F32), axis=0)
    grad = grad[:by_z] + grad[by_z:]
    grad = jnp.sum(exchange(to_all(grad, nodes), "node"), axis=0).astype(BF16)

    hits = lists[:, :, None] == my_x * mids + jnp.arange(mids, dtype=jnp.int32)
    hits = hits.transpose(0, 2, 1)[:, None, :, :, None]
    near = jnp.where(hits, edges[:, :, None], 0).sum(3).reshape(block, mids * block)
    product = got[:, 2 * by_z :].reshape(mids, strips, 2, 1, mine, block).transpose(0, 1, 3, 4, 2, 5)
    held = my_c == jnp.arange(cores).reshape(1, 1, cores, 1, 1, 1)
    product = jnp.where(held, product, 0).reshape(mids * block, 2 * block)
    logits = dot("rs,sc->rc", near, product).reshape(lanes, mine, 2 * block)
    logits = jnp.concatenate([logits[..., :block], logits[..., block:]], axis=1)

    grad = exchange(to_all(grad, blocks), "z").reshape(every, wide)[:kept]
    got = exchange(jnp.concatenate([to_all(grad, lanes), logits.astype(BF16)], axis=1), LANE)
    logits, grad = pl.pallas_call(
        finish,
        out_shape=(
            jax.ShapeDtypeStruct((mine, cls), F32),
            jax.ShapeDtypeStruct((cls, hid), F32),
        ),
        compiler_params=pltpu.CompilerParams(vmem_limit_bytes=16 * 2**20),
    )(got, own_logits)
    return rows, logits, grad.T


def solution(mesh):
    nodes = mesh.devices.shape[1]
    fine = Mesh(mesh.devices.reshape(4, 12, 2, nodes), ("x", "z", "c", "node"))
    col = ("x", "z", "c")
    rows = ("node", *col)
    in_specs = (
        P(col, "node"),
        P(None, col, None),
        P("node", None, None, None),
        P("node", None),
        P(rows, None, None),
        P("node", None),
        P(),
        P(rows, None),
    )
    out_specs = (P(rows, None), P(rows, None), P())
    return jax.shard_map(
        per_device, mesh=fine, in_specs=in_specs, out_specs=out_specs, check_vma=False
    )
```

```python
import functools

import jax
import jax.numpy as jnp
from jax import lax
from jax.experimental import pallas as pl
from jax.experimental.pallas import tpu as pltpu
from jax.sharding import Mesh, PartitionSpec as P

F32, BF16 = jnp.float32, jnp.bfloat16
LANE = ("x", "c")


def exchange(parts, axis):
    return lax.all_to_all(parts, axis, 0, 0, tiled=True)


def to_all(part, size):
    return jnp.broadcast_to(part[None], (size, *part.shape))


def dot(spec, a, b):
    return jnp.einsum(spec, a, b, preferred_element_type=F32)


def two(a):
    high = a.astype(BF16)
    return jnp.concatenate([high, (a - high.astype(F32)).astype(BF16)], axis=-2)


def near_rows(edges, cot, sends):
    rows, block = edges.shape
    mine, cls = cot.shape
    rest = jnp.concatenate([cot[:, block:], jnp.zeros((mine, 2 * block - cls), BF16)], axis=1)
    for j in range(sends.shape[0]):
        sends[j, :rows] = edges[...]
        sends[j, rows : rows + mine] = cot[:, :block]
        sends[j, rows + mine :] = rest


def first(xs, by_lane, spot, lists, got, agg, own, w, sends):
    lanes, _, block = got.shape
    blocks, cols = agg.shape[:2]
    listed = lists.shape[1]
    mids = blocks // xs
    strips = blocks // mids
    strip = block // strips
    mine = block // lanes
    edges = mine * listed
    total = lanes * edges
    over = (((1,), (1,)), ((), ()))
    cot = [got[:, edges : edges + mine], got[:, edges + mine :]]
    cot = jnp.concatenate([c.reshape(block, block) for c in cot], axis=1)
    shape = (by_lane, 2 * block)
    at = lax.broadcasted_iota(jnp.int32, shape, 1) - lax.broadcasted_iota(jnp.int32, shape, 0)
    pick = jnp.where(at == spot[1] * by_lane, 1.0, 0.0).astype(BF16)
    cot = lax.dot_general(pick, cot, over, preferred_element_type=F32).astype(BF16)
    row = lax.broadcasted_iota(jnp.int32, (block, total), 0)
    at = lax.broadcasted_iota(jnp.int32, (block, total), 1)
    spread = jnp.where(at // listed == row, 1.0, 0.0).astype(BF16)
    cot = jnp.dot(cot, spread, preferred_element_type=F32)
    at = lax.broadcasted_iota(jnp.int32, (by_lane, total), 1)
    to = jnp.full((by_lane, total), -1, jnp.int32)
    for x in range(xs):
        for k in range(listed):
            here = (at // (total // xs) == x) & (at % listed == k)
            to = jnp.where(here, lists[x * mids + spot[0], k], to)
    back = [jnp.where(to == b, cot, 0.0).astype(BF16) for b in range(blocks)]
    near = got[:, :edges].reshape(total, block)
    back = [jnp.dot(b, near, preferred_element_type=F32) for b in back]
    pad = jnp.zeros((sends.shape[1] - block - 2 * cols - by_lane, block), F32)
    parts = []
    for b in range(blocks):
        mine_b = own[:, b * block : (b + 1) * block].astype(F32)
        parts.append(jnp.concatenate([agg[b].astype(F32), mine_b, back[b], pad], axis=0))
    high = parts[0].shape[0]
    parts = [
        jnp.concatenate(parts[x * mids : (x + 1) * mids], axis=0).astype(BF16) for x in range(xs)
    ]
    parts = jnp.concatenate(parts, axis=1)
    row = lax.broadcasted_iota(jnp.int32, (xs * block, block), 0)
    to = lax.broadcasted_iota(jnp.int32, (xs * block, block), 1)
    fits = (to // strip == row // block) & (to % strip == row % strip)
    for low in range(strips):
        move = jnp.where(fits & (row % block // strip == low), 1.0, 0.0).astype(BF16)
        moved = jnp.dot(parts, move, preferred_element_type=F32).astype(BF16)
        for mid in range(mids):
            sends[mid * strips + low, :high] = moved[mid * high : (mid + 1) * high]
    wide = w.shape[2] // lanes
    w = [w[i, :, j * wide : (j + 1) * wide].astype(F32) for i in range(2) for j in range(lanes)]
    w = jnp.concatenate(w, axis=0).astype(BF16)
    for z in range(blocks):
        sends[z, high:] = w


def sum_nodes(got, sends):
    total = got[0]
    for n in range(1, got.shape[0]):
        total = total + got[n]
    for z in range(sends.shape[0]):
        sends[z] = total.astype(BF16)


def middle(got, w, sends, rows, logits):
    lanes, wide = got.shape[0], got.shape[2]
    blocks, by_z = sends.shape[0], sends.shape[1] // 4
    block, mine = got.shape[2], rows.shape[0]
    pre = got[0, : 2 * block].astype(F32)
    for j in range(1, lanes):
        pre = pre + got[j, : 2 * block].astype(F32)
    hidden = jnp.maximum(pre, 0.0).astype(BF16)
    for j in range(lanes):
        rows[:, j * wide : (j + 1) * wide] = hidden[block + j * mine : block + (j + 1) * mine]
    hidden = hidden[:block]
    back = got[:, 2 * block :].astype(F32)
    half = back.shape[1] // 2
    back = (back[:, :half] + back[:, half:]).reshape(lanes * half, block)
    high = back.astype(BF16)
    low = (back - high.astype(F32)).astype(BF16)
    grad = jnp.dot(high, hidden, preferred_element_type=F32)
    grad = grad + jnp.dot(low, hidden, preferred_element_type=F32)
    grad = grad.reshape(blocks, by_z, wide)
    high = grad.astype(BF16)
    sends[:, :by_z] = high
    sends[:, by_z : 2 * by_z] = (grad - high.astype(F32)).astype(BF16)
    over = (((1,), (1,)), ((), ()))
    product = lax.dot_general(rows[...], w[0], over, preferred_element_type=F32)
    logits[...] = lax.dot_general(rows[...], w[1], over, preferred_element_type=F32)
    pad = jnp.zeros((mine, 2 * block - product.shape[1]), F32)
    product = jnp.concatenate([product, pad], axis=1).astype(BF16)
    for z in range(blocks):
        sends[z, 2 * by_z : 2 * by_z + mine] = product[:, :block]
        sends[z, 2 * by_z + mine :] = product[:, block:]


def finish(got, own, logits, grad):
    lanes, wide = got.shape[0], got.shape[2]
    mine, cls = logits.shape
    kept = got.shape[1] - 2 * mine
    part = got[0, kept:].astype(F32)
    for j in range(1, lanes):
        part = part + got[j, kept:].astype(F32)
    part = jnp.concatenate([part[:mine], part[mine:]], axis=1)
    logits[...] = part[:, :cls] + own[...]
    for j in range(lanes):
        grad[:, j * wide : (j + 1) * wide] = got[j, :kept].astype(F32)[:cls]


def per_device(features, w_one, adj_one, list_one, adj_two, list_two, w_two, cotangent):
    cols, sources = features.shape
    blocks, fanout = list_one.shape
    block = adj_one.shape[-1]
    mine, listed = adj_two.shape[:2]
    hid, cls = w_two.shape[1:]
    nodes = lax.axis_size("node")
    xs, cores = lax.axis_size("x"), lax.axis_size("c")
    lanes = xs * cores
    wide = hid // lanes
    by_lane = -(-cls // (8 * lanes)) * 8
    every = by_lane * lanes
    by_z = every // blocks
    kept = -(-cls // 8) * 8
    strip = mine * cores
    strips = block // strip
    mids = blocks // xs
    place, my_x, my_c = (lax.axis_index(axis) for axis in ("z", "x", "c"))
    my_lane = my_x * cores + my_c
    mine_of = jnp.arange(blocks) == mids * jnp.arange(xs)[:, None] + place // strips
    lists = dot("xb,bk->xk", mine_of.astype(BF16), list_two.astype(BF16)).astype(jnp.int32)

    limit = pltpu.CompilerParams(vmem_limit_bytes=16 * 2**20)
    got = pl.pallas_call(
        near_rows,
        out_shape=jax.ShapeDtypeStruct((lanes, mine * (listed + 2), block), BF16),
        compiler_params=limit,
    )(adj_two.reshape(mine * listed, block), cotangent)
    near = exchange(got, LANE)
    edges = near[:, : mine * listed].reshape(xs, strip, listed, block)

    tiles = features.reshape(cols, sources // block, block)
    chosen = lax.gather(
        tiles,
        list_one.reshape(-1, 1),
        lax.GatherDimensionNumbers((0, 2), (1,), (1,)),
        (cols, 1, block),
        mode="promise_in_bounds",
    )
    chosen = chosen.reshape(cols, blocks, fanout, block)
    agg = dot("fhks,hkts->hft", chosen, adj_one).astype(BF16)
    above = -(-(2 * cols + by_lane) // 16) * 16
    whole = pl.BlockSpec(memory_space=pltpu.VMEM)
    scalars = pl.BlockSpec(memory_space=pltpu.SMEM)
    got = pl.pallas_call(
        functools.partial(first, xs, by_lane),
        grid=(1,),
        in_specs=[
            scalars,
            scalars,
            whole,
            whole,
            pl.BlockSpec((cols, blocks * block), lambda i: (0, 0)),
            whole,
        ],
        out_specs=whole,
        out_shape=jax.ShapeDtypeStruct((blocks, above + 2 * cols * lanes, block), BF16),
        compiler_params=limit,
    )(jnp.stack([place // strips, my_lane]), list_two, near, agg, features, w_one)
    got = exchange(got, "z")
    inputs, weights = got[:, : 2 * cols], got[:, above:]
    back = got[:, 2 * cols : 2 * cols + by_lane]
    inputs = inputs.reshape(blocks, 2, cols, block)
    weights = weights.reshape(blocks, 2, lanes, cols, wide)
    part = dot("zikr,zijkh->jrh", inputs, weights).astype(BF16)
    back = two(jnp.sum(back.astype(F32), axis=0))

    rows = part.reshape(lanes, lanes, mine, wide).transpose(1, 0, 2, 3)
    rows = rows.reshape(lanes, lanes * mine, wide)
    got = exchange(jnp.concatenate([part, rows, to_all(back, lanes)], axis=1), LANE)
    sends, rows, own_logits = pl.pallas_call(
        middle,
        out_shape=(
            jax.ShapeDtypeStruct((blocks, 4 * by_z, block), BF16),
            jax.ShapeDtypeStruct((mine, hid), BF16),
            jax.ShapeDtypeStruct((mine, cls), F32),
        ),
        compiler_params=limit,
    )(got, w_two.transpose(0, 2, 1))
    got = exchange(sends, "z")
    grad = jnp.sum(got[:, : 2 * by_z].astype(F32), axis=0)
    grad = grad[:by_z] + grad[by_z:]
    grad = pl.pallas_call(
        sum_nodes,
        out_shape=jax.ShapeDtypeStruct((blocks, by_z, wide), BF16),
        compiler_params=limit,
    )(exchange(to_all(grad, nodes), "node"))

    hits = lists[:, :, None] == my_x * mids + jnp.arange(mids, dtype=jnp.int32)
    hits = hits.transpose(0, 2, 1)[:, None, :, :, None]
    near = jnp.where(hits, edges[:, :, None], 0).sum(3).reshape(block, mids * block)
    product = got[:, 2 * by_z :].reshape(mids, strips, 2, 1, mine, block).transpose(0, 1, 3, 4, 2, 5)
    held = my_c == jnp.arange(cores).reshape(1, 1, cores, 1, 1, 1)
    product = jnp.where(held, product, 0).reshape(mids * block, 2 * block)
    logits = dot("rs,sc->rc", near, product).reshape(lanes, mine, 2 * block)
    logits = jnp.concatenate([logits[..., :block], logits[..., block:]], axis=1)

    grad = exchange(grad, "z").reshape(every, wide)[:kept]
    got = exchange(jnp.concatenate([to_all(grad, lanes), logits.astype(BF16)], axis=1), LANE)
    logits, grad = pl.pallas_call(
        finish,
        out_shape=(
            jax.ShapeDtypeStruct((mine, cls), F32),
            jax.ShapeDtypeStruct((cls, hid), F32),
        ),
        compiler_params=limit,
    )(got, own_logits)
    return rows, logits, grad.T


def solution(mesh):
    nodes = mesh.devices.shape[1]
    fine = Mesh(mesh.devices.reshape(4, 12, 2, nodes), ("x", "z", "c", "node"))
    col = ("x", "z", "c")
    rows = ("node", *col)
    in_specs = (
        P(col, "node"),
        P(None, col, None),
        P("node", None, None, None),
        P("node", None),
        P(rows, None, None),
        P("node", None),
        P(),
        P(rows, None),
    )
    out_specs = (P(rows, None), P(rows, None), P())
    return jax.shard_map(
        per_device, mesh=fine, in_specs=in_specs, out_specs=out_specs, check_vma=False
    )
```

```python
import functools

import jax
import jax.numpy as jnp
from jax import lax
from jax.experimental import pallas as pl
from jax.experimental.pallas import tpu as pltpu
from jax.sharding import Mesh, PartitionSpec as P

F32, BF16 = jnp.float32, jnp.bfloat16
LANE = ("x", "c")


def exchange(parts, axis):
    return lax.all_to_all(parts, axis, 0, 0, tiled=True)


def to_all(part, size):
    return jnp.broadcast_to(part[None], (size, *part.shape))


def dot(spec, a, b):
    return jnp.einsum(spec, a, b, preferred_element_type=F32)


def two(a):
    high = a.astype(BF16)
    return jnp.concatenate([high, (a - high.astype(F32)).astype(BF16)], axis=-2)


def near_rows(edges_in, cot_in, sends, edges, cot, sems):
    copies = [
        pltpu.make_async_copy(edges_in, edges, sems.at[0]),
        pltpu.make_async_copy(cot_in, cot, sems.at[1]),
    ]
    for copy in copies:
        copy.start()
    for copy in copies:
        copy.wait()
    rows, block = edges.shape
    mine, cls = cot.shape
    rest = jnp.concatenate([cot[:, block:], jnp.zeros((mine, 2 * block - cls), BF16)], axis=1)
    for j in range(sends.shape[0]):
        sends[j, :rows] = edges[...]
        sends[j, rows : rows + mine] = cot[:, :block]
        sends[j, rows + mine :] = rest


def first(xs, by_lane, spot, lists, got, agg_in, own, w_in, sends, agg, w, sems):
    copies = [
        pltpu.make_async_copy(agg_in, agg, sems.at[0]),
        pltpu.make_async_copy(w_in, w, sems.at[1]),
    ]
    for copy in copies:
        copy.start()
    lanes, _, block = got.shape
    blocks, cols = agg.shape[:2]
    listed = lists.shape[1]
    mids = blocks // xs
    strips = blocks // mids
    strip = block // strips
    mine = block // lanes
    edges = mine * listed
    total = lanes * edges
    over = (((1,), (1,)), ((), ()))
    cot = [got[:, edges : edges + mine], got[:, edges + mine :]]
    cot = jnp.concatenate([c.reshape(block, block) for c in cot], axis=1)
    shape = (by_lane, 2 * block)
    at = lax.broadcasted_iota(jnp.int32, shape, 1) - lax.broadcasted_iota(jnp.int32, shape, 0)
    pick = jnp.where(at == spot[1] * by_lane, 1.0, 0.0).astype(BF16)
    cot = lax.dot_general(pick, cot, over, preferred_element_type=F32).astype(BF16)
    row = lax.broadcasted_iota(jnp.int32, (block, total), 0)
    at = lax.broadcasted_iota(jnp.int32, (block, total), 1)
    spread = jnp.where(at // listed == row, 1.0, 0.0).astype(BF16)
    cot = jnp.dot(cot, spread, preferred_element_type=F32)
    at = lax.broadcasted_iota(jnp.int32, (by_lane, total), 1)
    to = jnp.full((by_lane, total), -1, jnp.int32)
    for x in range(xs):
        for k in range(listed):
            here = (at // (total // xs) == x) & (at % listed == k)
            to = jnp.where(here, lists[x * mids + spot[0], k], to)
    back = [jnp.where(to == b, cot, 0.0).astype(BF16) for b in range(blocks)]
    near = got[:, :edges].reshape(total, block)
    back = [jnp.dot(b, near, preferred_element_type=F32) for b in back]
    for copy in copies:
        copy.wait()
    pad = jnp.zeros((sends.shape[1] - block - 2 * cols - by_lane, block), F32)
    parts = []
    for b in range(blocks):
        mine_b = own[:, b * block : (b + 1) * block].astype(F32)
        parts.append(jnp.concatenate([agg[b].astype(F32), mine_b, back[b], pad], axis=0))
    high = parts[0].shape[0]
    parts = [
        jnp.concatenate(parts[x * mids : (x + 1) * mids], axis=0).astype(BF16) for x in range(xs)
    ]
    parts = jnp.concatenate(parts, axis=1)
    row = lax.broadcasted_iota(jnp.int32, (xs * block, block), 0)
    to = lax.broadcasted_iota(jnp.int32, (xs * block, block), 1)
    fits = (to // strip == row // block) & (to % strip == row % strip)
    for low in range(strips):
        move = jnp.where(fits & (row % block // strip == low), 1.0, 0.0).astype(BF16)
        moved = jnp.dot(parts, move, preferred_element_type=F32).astype(BF16)
        for mid in range(mids):
            sends[mid * strips + low, :high] = moved[mid * high : (mid + 1) * high]
    wide = w.shape[2] // lanes
    w = [w[i, :, j * wide : (j + 1) * wide].astype(F32) for i in range(2) for j in range(lanes)]
    w = jnp.concatenate(w, axis=0).astype(BF16)
    for z in range(blocks):
        sends[z, high:] = w


def sum_nodes(got, sends):
    total = got[0]
    for n in range(1, got.shape[0]):
        total = total + got[n]
    for z in range(sends.shape[0]):
        sends[z] = total.astype(BF16)


def middle(got, w_in, sends, rows, logits, w, sem):
    copy = pltpu.make_async_copy(w_in, w, sem)
    copy.start()
    lanes, wide = got.shape[0], got.shape[2]
    blocks, by_z = sends.shape[0], sends.shape[1] // 4
    block, mine = got.shape[2], rows.shape[0]
    pre = got[0, : 2 * block].astype(F32)
    for j in range(1, lanes):
        pre = pre + got[j, : 2 * block].astype(F32)
    hidden = jnp.maximum(pre, 0.0).astype(BF16)
    for j in range(lanes):
        rows[:, j * wide : (j + 1) * wide] = hidden[block + j * mine : block + (j + 1) * mine]
    hidden = hidden[:block]
    back = got[:, 2 * block :].astype(F32)
    half = back.shape[1] // 2
    back = (back[:, :half] + back[:, half:]).reshape(lanes * half, block)
    high = back.astype(BF16)
    low = (back - high.astype(F32)).astype(BF16)
    grad = jnp.dot(high, hidden, preferred_element_type=F32)
    grad = grad + jnp.dot(low, hidden, preferred_element_type=F32)
    grad = grad.reshape(blocks, by_z, wide)
    high = grad.astype(BF16)
    sends[:, :by_z] = high
    sends[:, by_z : 2 * by_z] = (grad - high.astype(F32)).astype(BF16)
    over = (((1,), (1,)), ((), ()))
    copy.wait()
    product = lax.dot_general(rows[...], w[0], over, preferred_element_type=F32)
    logits[...] = lax.dot_general(rows[...], w[1], over, preferred_element_type=F32)
    pad = jnp.zeros((mine, 2 * block - product.shape[1]), F32)
    product = jnp.concatenate([product, pad], axis=1).astype(BF16)
    for z in range(blocks):
        sends[z, 2 * by_z : 2 * by_z + mine] = product[:, :block]
        sends[z, 2 * by_z + mine :] = product[:, block:]


def sum_z(got, sends):
    by_z = sends.shape[1]
    total = got[0, : 2 * by_z].astype(F32)
    for z in range(1, got.shape[0]):
        total = total + got[z, : 2 * by_z].astype(F32)
    total = total[:by_z] + total[by_z:]
    for n in range(sends.shape[0]):
        sends[n] = total


def partial_logits(spot, got, near, sends):
    lanes, block = sends.shape[0], sends.shape[2]
    mine = sends.shape[1] // 2
    cores = near.shape[1] // (got.shape[0] * mine)
    above = got.shape[1] - 2 * mine
    rows = []
    for z in range(got.shape[0]):
        product = jnp.concatenate([got[z, above : above + mine], got[z, above + mine :]], axis=1)
        for c in range(cores):
            rows.append(jnp.where(spot[2] == c, product, jnp.zeros_like(product)))
    rows = jnp.concatenate(rows, axis=0)
    part = jnp.dot(near[...], rows, preferred_element_type=F32).astype(BF16)
    for j in range(lanes):
        sends[j, :mine] = part[j * mine : (j + 1) * mine, :block]
        sends[j, mine:] = part[j * mine : (j + 1) * mine, block:]


def finish(got, own, logits, grad):
    lanes, wide = got.shape[0], got.shape[2]
    mine, cls = logits.shape
    kept = got.shape[1] - 2 * mine
    part = got[0, kept:].astype(F32)
    for j in range(1, lanes):
        part = part + got[j, kept:].astype(F32)
    part = jnp.concatenate([part[:mine], part[mine:]], axis=1)
    logits[...] = part[:, :cls] + own[...]
    for j in range(lanes):
        grad[:, j * wide : (j + 1) * wide] = got[j, :kept].astype(F32)[:cls]


def per_device(features, w_one, adj_one, list_one, adj_two, list_two, w_two, cotangent):
    cols, sources = features.shape
    blocks, fanout = list_one.shape
    block = adj_one.shape[-1]
    mine, listed = adj_two.shape[:2]
    hid, cls = w_two.shape[1:]
    nodes = lax.axis_size("node")
    xs, cores = lax.axis_size("x"), lax.axis_size("c")
    lanes = xs * cores
    wide = hid // lanes
    by_lane = -(-cls // (8 * lanes)) * 8
    every = by_lane * lanes
    by_z = every // blocks
    kept = -(-cls // 8) * 8
    strip = mine * cores
    strips = block // strip
    mids = blocks // xs
    place, my_x, my_c = (lax.axis_index(axis) for axis in ("z", "x", "c"))
    my_lane = my_x * cores + my_c
    mine_of = jnp.arange(blocks) == mids * jnp.arange(xs)[:, None] + place // strips
    lists = dot("xb,bk->xk", mine_of.astype(BF16), list_two.astype(BF16)).astype(jnp.int32)

    limit = pltpu.CompilerParams(vmem_limit_bytes=16 * 2**20)
    wide_limit = pltpu.CompilerParams(vmem_limit_bytes=60 * 2**20)
    away = pl.BlockSpec(memory_space=pltpu.HBM)
    whole = pl.BlockSpec(memory_space=pltpu.VMEM)
    scalars = pl.BlockSpec(memory_space=pltpu.SMEM)
    got = pl.pallas_call(
        near_rows,
        in_specs=[away, away],
        out_shape=jax.ShapeDtypeStruct((lanes, mine * (listed + 2), block), BF16),
        scratch_shapes=[
            pltpu.VMEM((mine * listed, block), BF16),
            pltpu.VMEM((mine, cls), BF16),
            pltpu.SemaphoreType.DMA((2,)),
        ],
        compiler_params=limit,
    )(adj_two.reshape(mine * listed, block), cotangent)
    near = exchange(got, LANE)
    edges = near[:, : mine * listed].reshape(xs, strip, listed, block)

    tiles = features.reshape(cols, sources // block, block)
    chosen = lax.gather(
        tiles,
        list_one.reshape(-1, 1),
        lax.GatherDimensionNumbers((0, 2), (1,), (1,)),
        (cols, 1, block),
        mode="promise_in_bounds",
    )
    chosen = chosen.reshape(cols, blocks, fanout, block)
    agg = dot("fhks,hkts->hft", chosen, adj_one).astype(BF16)
    above = -(-(2 * cols + by_lane) // 16) * 16
    spot = jnp.stack([place // strips, my_lane, my_c])
    got = pl.pallas_call(
        functools.partial(first, xs, by_lane),
        grid=(1,),
        in_specs=[
            scalars,
            scalars,
            whole,
            away,
            pl.BlockSpec((cols, blocks * block), lambda i: (0, 0)),
            away,
        ],
        out_specs=whole,
        out_shape=jax.ShapeDtypeStruct((blocks, above + 2 * cols * lanes, block), BF16),
        scratch_shapes=[
            pltpu.VMEM(agg.shape, BF16),
            pltpu.VMEM(w_one.shape, BF16),
            pltpu.SemaphoreType.DMA((2,)),
        ],
        compiler_params=wide_limit,
    )(spot, list_two, near, agg, features, w_one)
    got = exchange(got, "z")
    inputs, weights = got[:, : 2 * cols], got[:, above:]
    back = got[:, 2 * cols : 2 * cols + by_lane]
    inputs = inputs.reshape(blocks, 2, cols, block)
    weights = weights.reshape(blocks, 2, lanes, cols, wide)
    part = dot("zikr,zijkh->jrh", inputs, weights).astype(BF16)
    back = two(jnp.sum(back.astype(F32), axis=0))

    rows = part.reshape(lanes, lanes, mine, wide).transpose(1, 0, 2, 3)
    rows = rows.reshape(lanes, lanes * mine, wide)
    got = exchange(jnp.concatenate([part, rows, to_all(back, lanes)], axis=1), LANE)
    sends, rows, own_logits = pl.pallas_call(
        middle,
        in_specs=[whole, away],
        scratch_shapes=[pltpu.VMEM((2, cls, hid), BF16), pltpu.SemaphoreType.DMA],
        out_shape=(
            jax.ShapeDtypeStruct((blocks, 4 * by_z, block), BF16),
            jax.ShapeDtypeStruct((mine, hid), BF16),
            jax.ShapeDtypeStruct((mine, cls), F32),
        ),
        compiler_params=wide_limit,
    )(got, w_two.transpose(0, 2, 1))
    got = exchange(sends, "z")
    grad = pl.pallas_call(
        sum_z,
        out_shape=jax.ShapeDtypeStruct((nodes, by_z, wide), F32),
        compiler_params=limit,
    )(got)
    grad = pl.pallas_call(
        sum_nodes,
        out_shape=jax.ShapeDtypeStruct((blocks, by_z, wide), BF16),
        compiler_params=limit,
    )(exchange(grad, "node"))

    hits = lists[:, :, None] == my_x * mids + jnp.arange(mids, dtype=jnp.int32)
    hits = hits.transpose(0, 2, 1)[:, None, :, :, None]
    near = jnp.where(hits, edges[:, :, None], 0).sum(3).reshape(block, mids * block)
    logits = pl.pallas_call(
        partial_logits,
        in_specs=[scalars, whole, whole],
        out_shape=jax.ShapeDtypeStruct((lanes, 2 * mine, block), BF16),
        compiler_params=limit,
    )(spot, got, near)

    grad = exchange(grad, "z").reshape(every, wide)[:kept]
    got = exchange(jnp.concatenate([to_all(grad, lanes), logits], axis=1), LANE)
    logits, grad = pl.pallas_call(
        finish,
        out_shape=(
            jax.ShapeDtypeStruct((mine, cls), F32),
            jax.ShapeDtypeStruct((cls, hid), F32),
        ),
        compiler_params=limit,
    )(got, own_logits)
    return rows, logits, grad.T


def solution(mesh):
    nodes = mesh.devices.shape[1]
    fine = Mesh(mesh.devices.reshape(4, 12, 2, nodes), ("x", "z", "c", "node"))
    col = ("x", "z", "c")
    rows = ("node", *col)
    in_specs = (
        P(col, "node"),
        P(None, col, None),
        P("node", None, None, None),
        P("node", None),
        P(rows, None, None),
        P("node", None),
        P(),
        P(rows, None),
    )
    out_specs = (P(rows, None), P(rows, None), P())
    return jax.shard_map(
        per_device, mesh=fine, in_specs=in_specs, out_specs=out_specs, check_vma=False
    )
```

```python
import functools

import jax
import jax.numpy as jnp
from jax import lax
from jax.experimental import pallas as pl
from jax.experimental.pallas import tpu as pltpu
from jax.sharding import Mesh, PartitionSpec as P

F32, BF16 = jnp.float32, jnp.bfloat16
LANE = ("x", "c")


def exchange(parts, axis):
    return lax.all_to_all(parts, axis, 0, 0, tiled=True)


def to_all(part, size):
    return jnp.broadcast_to(part[None], (size, *part.shape))


def dot(spec, a, b):
    return jnp.einsum(spec, a, b, preferred_element_type=F32)


def two(a):
    high = a.astype(BF16)
    return jnp.concatenate([high, (a - high.astype(F32)).astype(BF16)], axis=-2)


def near_rows(edges_in, cot_in, sends, edges, cot, sems):
    copies = [
        pltpu.make_async_copy(edges_in, edges, sems.at[0]),
        pltpu.make_async_copy(cot_in, cot, sems.at[1]),
    ]
    for copy in copies:
        copy.start()
    for copy in copies:
        copy.wait()
    rows, block = edges.shape
    mine, cls = cot.shape
    rest = jnp.concatenate([cot[:, block:], jnp.zeros((mine, 2 * block - cls), BF16)], axis=1)
    for j in range(sends.shape[0]):
        sends[j, :rows] = edges[...]
        sends[j, rows : rows + mine] = cot[:, :block]
        sends[j, rows + mine :] = rest


def first(xs, by_lane, lists, got, agg_in, own, w_in, sends, edges_out, agg, w, sems):
    copies = [
        pltpu.make_async_copy(agg_in, agg, sems.at[0]),
        pltpu.make_async_copy(w_in, w, sems.at[1]),
    ]
    for copy in copies:
        copy.start()
    lanes, _, block = got.shape
    blocks, cols = agg.shape[:2]
    listed = lists.shape[0]
    mids = blocks // xs
    strips = blocks // mids
    strip = block // strips
    mine = block // lanes
    my_x, my_mid = lax.axis_index("x"), lax.axis_index("z") // strips
    my_lane = my_x * (lanes // xs) + lax.axis_index("c")
    edges = mine * listed
    total = lanes * edges
    over = (((1,), (1,)), ((), ()))
    cot = [got[:, edges : edges + mine], got[:, edges + mine :]]
    cot = jnp.concatenate([c.reshape(block, block) for c in cot], axis=1)
    shape = (by_lane, 2 * block)
    at = lax.broadcasted_iota(jnp.int32, shape, 1) - lax.broadcasted_iota(jnp.int32, shape, 0)
    pick = jnp.where(at == my_lane * by_lane, 1.0, 0.0).astype(BF16)
    cot = lax.dot_general(pick, cot, over, preferred_element_type=F32).astype(BF16)
    row = lax.broadcasted_iota(jnp.int32, (block, total), 0)
    at = lax.broadcasted_iota(jnp.int32, (block, total), 1)
    fits = at // listed == row
    spread = jnp.where(fits, 1.0, 0.0).astype(BF16)
    cot = jnp.dot(cot, spread, preferred_element_type=F32)
    at = lax.broadcasted_iota(jnp.int32, (8, total), 1)
    to = jnp.full((8, total), -1, jnp.int32)
    for x in range(xs):
        for k in range(listed):
            here = (at // (total // xs) == x) & (at % listed == k)
            to = jnp.where(here, lists[k, x * mids + my_mid], to)
    to = jnp.concatenate([to] * (block // 8), axis=0)
    back = [jnp.where(to[:by_lane] == b, cot, 0.0).astype(BF16) for b in range(blocks)]
    near = got[:, :edges].reshape(total, block)
    back = [jnp.dot(b, near, preferred_element_type=F32) for b in back]
    for mid in range(mids):
        take = jnp.where(fits & (to == my_x * mids + mid), 1.0, 0.0).astype(BF16)
        take = jnp.dot(take, near, preferred_element_type=F32).astype(BF16)
        edges_out[:, mid * block : (mid + 1) * block] = take
    for copy in copies:
        copy.wait()
    pad = jnp.zeros((sends.shape[1] - block - 2 * cols - by_lane, block), F32)
    parts = []
    for b in range(blocks):
        mine_b = own[:, b * block : (b + 1) * block].astype(F32)
        parts.append(jnp.concatenate([agg[b].astype(F32), mine_b, back[b], pad], axis=0))
    high = parts[0].shape[0]
    parts = [
        jnp.concatenate(parts[x * mids : (x + 1) * mids], axis=0).astype(BF16) for x in range(xs)
    ]
    parts = jnp.concatenate(parts, axis=1)
    row = lax.broadcasted_iota(jnp.int32, (xs * block, block), 0)
    to = lax.broadcasted_iota(jnp.int32, (xs * block, block), 1)
    fits = (to // strip == row // block) & (to % strip == row % strip)
    for low in range(strips):
        move = jnp.where(fits & (row % block // strip == low), 1.0, 0.0).astype(BF16)
        moved = jnp.dot(parts, move, preferred_element_type=F32).astype(BF16)
        for mid in range(mids):
            sends[mid * strips + low, :high] = moved[mid * high : (mid + 1) * high]
    wide = w.shape[2] // lanes
    w = [w[i, :, j * wide : (j + 1) * wide].astype(F32) for i in range(2) for j in range(lanes)]
    w = jnp.concatenate(w, axis=0).astype(BF16)
    for z in range(blocks):
        sends[z, high:] = w


def sum_nodes(got, sends):
    total = got[0]
    for n in range(1, got.shape[0]):
        total = total + got[n]
    for z in range(sends.shape[0]):
        sends[z] = total.astype(BF16)


def middle(got, w_in, sends, rows, logits, w, sem):
    copy = pltpu.make_async_copy(w_in, w, sem)
    copy.start()
    lanes, wide = got.shape[0], got.shape[2]
    blocks, by_z = sends.shape[0], sends.shape[1] // 4
    block, mine = got.shape[2], rows.shape[0]
    pre = got[0, : 2 * block].astype(F32)
    for j in range(1, lanes):
        pre = pre + got[j, : 2 * block].astype(F32)
    hidden = jnp.maximum(pre, 0.0).astype(BF16)
    for j in range(lanes):
        rows[:, j * wide : (j + 1) * wide] = hidden[block + j * mine : block + (j + 1) * mine]
    hidden = hidden[:block]
    back = got[:, 2 * block :].astype(F32)
    half = back.shape[1] // 2
    back = (back[:, :half] + back[:, half:]).reshape(lanes * half, block)
    high = back.astype(BF16)
    low = (back - high.astype(F32)).astype(BF16)
    grad = jnp.dot(high, hidden, preferred_element_type=F32)
    grad = grad + jnp.dot(low, hidden, preferred_element_type=F32)
    grad = grad.reshape(blocks, by_z, wide)
    high = grad.astype(BF16)
    sends[:, :by_z] = high
    sends[:, by_z : 2 * by_z] = (grad - high.astype(F32)).astype(BF16)
    over = (((1,), (1,)), ((), ()))
    copy.wait()
    product = lax.dot_general(rows[...], w[0], over, preferred_element_type=F32)
    logits[...] = lax.dot_general(rows[...], w[1], over, preferred_element_type=F32)
    pad = jnp.zeros((mine, 2 * block - product.shape[1]), F32)
    product = jnp.concatenate([product, pad], axis=1).astype(BF16)
    for z in range(blocks):
        sends[z, 2 * by_z : 2 * by_z + mine] = product[:, :block]
        sends[z, 2 * by_z + mine :] = product[:, block:]


def sum_z(got, sends):
    by_z = sends.shape[1]
    total = got[0, : 2 * by_z].astype(F32)
    for z in range(1, got.shape[0]):
        total = total + got[z, : 2 * by_z].astype(F32)
    total = total[:by_z] + total[by_z:]
    for n in range(sends.shape[0]):
        sends[n] = total


def partial_logits(got, near, sends):
    lanes, block = sends.shape[0], sends.shape[2]
    mine = sends.shape[1] // 2
    cores = near.shape[1] // (got.shape[0] * mine)
    above = got.shape[1] - 2 * mine
    my_c = lax.axis_index("c")
    rows = []
    for z in range(got.shape[0]):
        product = jnp.concatenate([got[z, above : above + mine], got[z, above + mine :]], axis=1)
        for c in range(cores):
            rows.append(jnp.where(my_c == c, product, jnp.zeros_like(product)))
    rows = jnp.concatenate(rows, axis=0)
    part = jnp.dot(near[...], rows, preferred_element_type=F32).astype(BF16)
    for j in range(lanes):
        sends[j, :mine] = part[j * mine : (j + 1) * mine, :block]
        sends[j, mine:] = part[j * mine : (j + 1) * mine, block:]


def last(grad, logits, sends):
    kept = sends.shape[1] - logits.shape[1]
    by_z = grad.shape[1]
    for j in range(sends.shape[0]):
        for z in range(kept // by_z):
            sends[j, z * by_z : (z + 1) * by_z] = grad[z]
        sends[j, kept:] = logits[j]


def finish(got, own, logits, grad):
    lanes, wide = got.shape[0], got.shape[2]
    mine, cls = logits.shape
    kept = got.shape[1] - 2 * mine
    part = got[0, kept:].astype(F32)
    for j in range(1, lanes):
        part = part + got[j, kept:].astype(F32)
    part = jnp.concatenate([part[:mine], part[mine:]], axis=1)
    logits[...] = part[:, :cls] + own[...]
    for j in range(lanes):
        grad[:, j * wide : (j + 1) * wide] = got[j, :kept].astype(F32)[:cls]


def per_device(features, w_one, adj_one, list_one, adj_two, list_two, w_two, cotangent):
    cols, sources = features.shape
    blocks, fanout = list_one.shape
    block = adj_one.shape[-1]
    mine, listed = adj_two.shape[:2]
    hid, cls = w_two.shape[1:]
    nodes = lax.axis_size("node")
    xs, cores = lax.axis_size("x"), lax.axis_size("c")
    lanes = xs * cores
    wide = hid // lanes
    by_lane = -(-cls // (8 * lanes)) * 8
    every = by_lane * lanes
    by_z = every // blocks
    kept = -(-cls // 8) * 8
    strip = mine * cores
    strips = block // strip
    mids = blocks // xs
    limit = pltpu.CompilerParams(vmem_limit_bytes=16 * 2**20)
    wide_limit = pltpu.CompilerParams(vmem_limit_bytes=60 * 2**20)
    away = pl.BlockSpec(memory_space=pltpu.HBM)
    whole = pl.BlockSpec(memory_space=pltpu.VMEM)
    scalars = pl.BlockSpec(memory_space=pltpu.SMEM)
    got = pl.pallas_call(
        near_rows,
        in_specs=[away, away],
        out_shape=jax.ShapeDtypeStruct((lanes, mine * (listed + 2), block), BF16),
        scratch_shapes=[
            pltpu.VMEM((mine * listed, block), BF16),
            pltpu.VMEM((mine, cls), BF16),
            pltpu.SemaphoreType.DMA((2,)),
        ],
        compiler_params=wide_limit,
    )(adj_two.reshape(mine * listed, block), cotangent)
    near = exchange(got, LANE)

    tiles = features.reshape(cols, sources // block, block)
    chosen = lax.gather(
        tiles,
        list_one.reshape(-1, 1),
        lax.GatherDimensionNumbers((0, 2), (1,), (1,)),
        (cols, 1, block),
        mode="promise_in_bounds",
    )
    chosen = chosen.reshape(cols, blocks, fanout, block)
    agg = dot("fhks,hkts->hft", chosen, adj_one).astype(BF16)
    above = -(-(2 * cols + by_lane) // 16) * 16
    got, near = pl.pallas_call(
        functools.partial(first, xs, by_lane),
        grid=(1,),
        in_specs=[
            scalars,
            whole,
            away,
            pl.BlockSpec((cols, blocks * block), lambda i: (0, 0)),
            away,
        ],
        out_specs=(whole, whole),
        out_shape=(
            jax.ShapeDtypeStruct((blocks, above + 2 * cols * lanes, block), BF16),
            jax.ShapeDtypeStruct((block, mids * block), BF16),
        ),
        scratch_shapes=[
            pltpu.VMEM(agg.shape, BF16),
            pltpu.VMEM(w_one.shape, BF16),
            pltpu.SemaphoreType.DMA((2,)),
        ],
        compiler_params=wide_limit,
    )(list_two.T, near, agg, features, w_one)
    got = exchange(got, "z")
    inputs, weights = got[:, : 2 * cols], got[:, above:]
    back = got[:, 2 * cols : 2 * cols + by_lane]
    inputs = inputs.reshape(blocks, 2, cols, block)
    weights = weights.reshape(blocks, 2, lanes, cols, wide)
    part = dot("zikr,zijkh->jrh", inputs, weights).astype(BF16)
    back = two(jnp.sum(back.astype(F32), axis=0))

    rows = part.reshape(lanes, lanes, mine, wide).transpose(1, 0, 2, 3)
    rows = rows.reshape(lanes, lanes * mine, wide)
    got = exchange(jnp.concatenate([part, rows, to_all(back, lanes)], axis=1), LANE)
    sends, rows, own_logits = pl.pallas_call(
        middle,
        in_specs=[whole, away],
        scratch_shapes=[pltpu.VMEM((2, cls, hid), BF16), pltpu.SemaphoreType.DMA],
        out_shape=(
            jax.ShapeDtypeStruct((blocks, 4 * by_z, block), BF16),
            jax.ShapeDtypeStruct((mine, hid), BF16),
            jax.ShapeDtypeStruct((mine, cls), F32),
        ),
        compiler_params=wide_limit,
    )(got, w_two.transpose(0, 2, 1))
    got = exchange(sends, "z")
    grad = pl.pallas_call(
        sum_z,
        out_shape=jax.ShapeDtypeStruct((nodes, by_z, wide), F32),
        compiler_params=limit,
    )(got)
    grad = pl.pallas_call(
        sum_nodes,
        out_shape=jax.ShapeDtypeStruct((blocks, by_z, wide), BF16),
        compiler_params=limit,
    )(exchange(grad, "node"))

    logits = pl.pallas_call(
        partial_logits,
        in_specs=[whole, whole],
        out_shape=jax.ShapeDtypeStruct((lanes, 2 * mine, block), BF16),
        compiler_params=limit,
    )(got, near)

    got = pl.pallas_call(
        last,
        out_shape=jax.ShapeDtypeStruct((lanes, kept + 2 * mine, block), BF16),
        compiler_params=limit,
    )(exchange(grad, "z"), logits)
    got = exchange(got, LANE)
    logits, grad = pl.pallas_call(
        finish,
        out_shape=(
            jax.ShapeDtypeStruct((mine, cls), F32),
            jax.ShapeDtypeStruct((cls, hid), F32),
        ),
        compiler_params=limit,
    )(got, own_logits)
    return rows, logits, grad.T


def solution(mesh):
    nodes = mesh.devices.shape[1]
    fine = Mesh(mesh.devices.reshape(4, 12, 2, nodes), ("x", "z", "c", "node"))
    col = ("x", "z", "c")
    rows = ("node", *col)
    in_specs = (
        P(col, "node"),
        P(None, col, None),
        P("node", None, None, None),
        P("node", None),
        P(rows, None, None),
        P("node", None),
        P(),
        P(rows, None),
    )
    out_specs = (P(rows, None), P(rows, None), P())
    return jax.shard_map(
        per_device, mesh=fine, in_specs=in_specs, out_specs=out_specs, check_vma=False
    )
```

```python
import functools

import jax
import jax.numpy as jnp
from jax import lax
from jax.experimental import pallas as pl
from jax.experimental.pallas import tpu as pltpu
from jax.sharding import Mesh, PartitionSpec as P

F32, BF16 = jnp.float32, jnp.bfloat16
LANE = ("x", "c")


def exchange(parts, axis):
    return lax.all_to_all(parts, axis, 0, 0, tiled=True)


def to_all(part, size):
    return jnp.broadcast_to(part[None], (size, *part.shape))


def dot(spec, a, b):
    return jnp.einsum(spec, a, b, preferred_element_type=F32)


def two(a):
    high = a.astype(BF16)
    return jnp.concatenate([high, (a - high.astype(F32)).astype(BF16)], axis=-2)


def near_rows(edges_in, cot_in, sends, edges, cot, sems):
    copies = [
        pltpu.make_async_copy(edges_in, edges, sems.at[0]),
        pltpu.make_async_copy(cot_in, cot, sems.at[1]),
    ]
    for copy in copies:
        copy.start()
    for copy in copies:
        copy.wait()
    rows, block = edges.shape
    mine, cls = cot.shape
    rest = jnp.concatenate([cot[:, block:], jnp.zeros((mine, 2 * block - cls), BF16)], axis=1)
    for j in range(sends.shape[0]):
        sends[j, :rows] = edges[...]
        sends[j, rows : rows + mine] = cot[:, :block]
        sends[j, rows + mine :] = rest


def pick_blocks(lists, tiles_in, chosen, tiles, sem):
    copy = pltpu.make_async_copy(tiles_in, tiles, sem)
    copy.start()
    copy.wait()
    fanout, blocks = lists.shape
    block = chosen.shape[2]
    for b in range(blocks):
        for k in range(fanout):
            at = pl.multiple_of(lists[k, b] * block, block)
            chosen[b * fanout + k] = tiles[:, pl.ds(at, block)]


def first(xs, by_lane, lists, got, agg_in, own, w_in, sends, edges_out, agg, w, sems):
    copies = [
        pltpu.make_async_copy(agg_in, agg, sems.at[0]),
        pltpu.make_async_copy(w_in, w, sems.at[1]),
    ]
    for copy in copies:
        copy.start()
    lanes, _, block = got.shape
    blocks, cols = agg.shape[:2]
    listed = lists.shape[0]
    mids = blocks // xs
    strips = blocks // mids
    strip = block // strips
    mine = block // lanes
    my_x, my_mid = lax.axis_index("x"), lax.axis_index("z") // strips
    my_lane = my_x * (lanes // xs) + lax.axis_index("c")
    edges = mine * listed
    total = lanes * edges
    over = (((1,), (1,)), ((), ()))
    cot = [got[:, edges : edges + mine], got[:, edges + mine :]]
    cot = jnp.concatenate([c.reshape(block, block) for c in cot], axis=1)
    shape = (by_lane, 2 * block)
    at = lax.broadcasted_iota(jnp.int32, shape, 1) - lax.broadcasted_iota(jnp.int32, shape, 0)
    pick = jnp.where(at == my_lane * by_lane, 1.0, 0.0).astype(BF16)
    cot = lax.dot_general(pick, cot, over, preferred_element_type=F32).astype(BF16)
    row = lax.broadcasted_iota(jnp.int32, (block, total), 0)
    at = lax.broadcasted_iota(jnp.int32, (block, total), 1)
    fits = at // listed == row
    spread = jnp.where(fits, 1.0, 0.0).astype(BF16)
    cot = jnp.dot(cot, spread, preferred_element_type=F32)
    at = lax.broadcasted_iota(jnp.int32, (8, total), 1)
    to = jnp.full((8, total), -1, jnp.int32)
    for x in range(xs):
        for k in range(listed):
            here = (at // (total // xs) == x) & (at % listed == k)
            to = jnp.where(here, lists[k, x * mids + my_mid], to)
    to = jnp.concatenate([to] * (block // 8), axis=0)
    back = [jnp.where(to[:by_lane] == b, cot, 0.0).astype(BF16) for b in range(blocks)]
    near = got[:, :edges].reshape(total, block)
    back = [jnp.dot(b, near, preferred_element_type=F32) for b in back]
    for mid in range(mids):
        take = jnp.where(fits & (to == my_x * mids + mid), 1.0, 0.0).astype(BF16)
        take = jnp.dot(take, near, preferred_element_type=F32).astype(BF16)
        edges_out[:, mid * block : (mid + 1) * block] = take
    for copy in copies:
        copy.wait()
    pad = jnp.zeros((sends.shape[1] - block - 2 * cols - by_lane, block), F32)
    parts = []
    for b in range(blocks):
        mine_b = own[:, b * block : (b + 1) * block].astype(F32)
        parts.append(jnp.concatenate([agg[b].astype(F32), mine_b, back[b], pad], axis=0))
    high = parts[0].shape[0]
    parts = [
        jnp.concatenate(parts[x * mids : (x + 1) * mids], axis=0).astype(BF16) for x in range(xs)
    ]
    parts = jnp.concatenate(parts, axis=1)
    row = lax.broadcasted_iota(jnp.int32, (xs * block, block), 0)
    to = lax.broadcasted_iota(jnp.int32, (xs * block, block), 1)
    fits = (to // strip == row // block) & (to % strip == row % strip)
    for low in range(strips):
        move = jnp.where(fits & (row % block // strip == low), 1.0, 0.0).astype(BF16)
        moved = jnp.dot(parts, move, preferred_element_type=F32).astype(BF16)
        for mid in range(mids):
            sends[mid * strips + low, :high] = moved[mid * high : (mid + 1) * high]
    wide = w.shape[2] // lanes
    w = [w[i, :, j * wide : (j + 1) * wide].astype(F32) for i in range(2) for j in range(lanes)]
    w = jnp.concatenate(w, axis=0).astype(BF16)
    for z in range(blocks):
        sends[z, high:] = w


def sum_nodes(got, sends):
    total = got[0]
    for n in range(1, got.shape[0]):
        total = total + got[n]
    for z in range(sends.shape[0]):
        sends[z] = total.astype(BF16)


def middle(got, w_in, sends, rows, logits, w, sem):
    copy = pltpu.make_async_copy(w_in, w, sem)
    copy.start()
    lanes, wide = got.shape[0], got.shape[2]
    blocks, by_z = sends.shape[0], sends.shape[1] // 4
    block, mine = got.shape[2], rows.shape[0]
    pre = got[0, : 2 * block].astype(F32)
    for j in range(1, lanes):
        pre = pre + got[j, : 2 * block].astype(F32)
    hidden = jnp.maximum(pre, 0.0).astype(BF16)
    for j in range(lanes):
        rows[:, j * wide : (j + 1) * wide] = hidden[block + j * mine : block + (j + 1) * mine]
    hidden = hidden[:block]
    back = got[:, 2 * block :].astype(F32)
    half = back.shape[1] // 2
    back = (back[:, :half] + back[:, half:]).reshape(lanes * half, block)
    high = back.astype(BF16)
    low = (back - high.astype(F32)).astype(BF16)
    grad = jnp.dot(high, hidden, preferred_element_type=F32)
    grad = grad + jnp.dot(low, hidden, preferred_element_type=F32)
    grad = grad.reshape(blocks, by_z, wide)
    high = grad.astype(BF16)
    sends[:, :by_z] = high
    sends[:, by_z : 2 * by_z] = (grad - high.astype(F32)).astype(BF16)
    over = (((1,), (1,)), ((), ()))
    copy.wait()
    product = lax.dot_general(rows[...], w[0], over, preferred_element_type=F32)
    logits[...] = lax.dot_general(rows[...], w[1], over, preferred_element_type=F32)
    pad = jnp.zeros((mine, 2 * block - product.shape[1]), F32)
    product = jnp.concatenate([product, pad], axis=1).astype(BF16)
    for z in range(blocks):
        sends[z, 2 * by_z : 2 * by_z + mine] = product[:, :block]
        sends[z, 2 * by_z + mine :] = product[:, block:]


def sum_z(got, sends):
    by_z = sends.shape[1]
    total = got[0, : 2 * by_z].astype(F32)
    for z in range(1, got.shape[0]):
        total = total + got[z, : 2 * by_z].astype(F32)
    total = total[:by_z] + total[by_z:]
    for n in range(sends.shape[0]):
        sends[n] = total


def partial_logits(got, near, own_in, sends, own):
    lanes, block = sends.shape[0], sends.shape[2]
    mine = sends.shape[1] // 2
    cores = near.shape[1] // (got.shape[0] * mine)
    above = got.shape[1] - 2 * mine
    my_c = lax.axis_index("c")
    own[...] = own_in[...]
    rows = []
    for z in range(got.shape[0]):
        product = jnp.concatenate([got[z, above : above + mine], got[z, above + mine :]], axis=1)
        for c in range(cores):
            rows.append(jnp.where(my_c == c, product, jnp.zeros_like(product)))
    rows = jnp.concatenate(rows, axis=0)
    part = jnp.dot(near[...], rows, preferred_element_type=F32).astype(BF16)
    for j in range(lanes):
        sends[j, :mine] = part[j * mine : (j + 1) * mine, :block]
        sends[j, mine:] = part[j * mine : (j + 1) * mine, block:]


def last(grad, logits, sends):
    kept = sends.shape[1] - logits.shape[1]
    by_z = grad.shape[1]
    for j in range(sends.shape[0]):
        for z in range(kept // by_z):
            sends[j, z * by_z : (z + 1) * by_z] = grad[z]
        sends[j, kept:] = logits[j]


def finish(got, own, logits, grad):
    lanes, wide = got.shape[0], got.shape[2]
    mine, cls = logits.shape
    kept = got.shape[1] - 2 * mine
    part = got[0, kept:].astype(F32)
    for j in range(1, lanes):
        part = part + got[j, kept:].astype(F32)
    part = jnp.concatenate([part[:mine], part[mine:]], axis=1)
    logits[...] = part[:, :cls] + own[...]
    for j in range(lanes):
        grad[:, j * wide : (j + 1) * wide] = got[j, :kept].astype(F32)[:cls]


def per_device(features, w_one, adj_one, list_one, adj_two, list_two, w_two, cotangent):
    cols, sources = features.shape
    blocks, fanout = list_one.shape
    block = adj_one.shape[-1]
    mine, listed = adj_two.shape[:2]
    hid, cls = w_two.shape[1:]
    nodes = lax.axis_size("node")
    xs, cores = lax.axis_size("x"), lax.axis_size("c")
    lanes = xs * cores
    wide = hid // lanes
    by_lane = -(-cls // (8 * lanes)) * 8
    every = by_lane * lanes
    by_z = every // blocks
    kept = -(-cls // 8) * 8
    strip = mine * cores
    strips = block // strip
    mids = blocks // xs
    limit = pltpu.CompilerParams(vmem_limit_bytes=16 * 2**20)
    wide_limit = pltpu.CompilerParams(vmem_limit_bytes=60 * 2**20)
    away = pl.BlockSpec(memory_space=pltpu.HBM)
    whole = pl.BlockSpec(memory_space=pltpu.VMEM)
    scalars = pl.BlockSpec(memory_space=pltpu.SMEM)
    got = pl.pallas_call(
        near_rows,
        in_specs=[away, away],
        out_shape=jax.ShapeDtypeStruct((lanes, mine * (listed + 2), block), BF16),
        scratch_shapes=[
            pltpu.VMEM((mine * listed, block), BF16),
            pltpu.VMEM((mine, cls), BF16),
            pltpu.SemaphoreType.DMA((2,)),
        ],
        compiler_params=wide_limit,
    )(adj_two.reshape(mine * listed, block), cotangent)
    near = exchange(got, LANE)

    chosen = pl.pallas_call(
        pick_blocks,
        in_specs=[scalars, away],
        out_shape=jax.ShapeDtypeStruct((blocks * fanout, cols, block), BF16),
        scratch_shapes=[pltpu.VMEM((cols, sources), BF16), pltpu.SemaphoreType.DMA],
        compiler_params=limit,
    )(list_one.T, features)
    chosen = chosen.reshape(blocks, fanout, cols, block)
    agg = dot("hkfs,hkts->hft", chosen, adj_one).astype(BF16)
    above = -(-(2 * cols + by_lane) // 16) * 16
    got, near = pl.pallas_call(
        functools.partial(first, xs, by_lane),
        grid=(1,),
        in_specs=[
            scalars,
            whole,
            away,
            pl.BlockSpec((cols, blocks * block), lambda i: (0, 0)),
            away,
        ],
        out_specs=(whole, whole),
        out_shape=(
            jax.ShapeDtypeStruct((blocks, above + 2 * cols * lanes, block), BF16),
            jax.ShapeDtypeStruct((block, mids * block), BF16),
        ),
        scratch_shapes=[
            pltpu.VMEM(agg.shape, BF16),
            pltpu.VMEM(w_one.shape, BF16),
            pltpu.SemaphoreType.DMA((2,)),
        ],
        compiler_params=wide_limit,
    )(list_two.T, near, agg, features, w_one)
    got = exchange(got, "z")
    inputs, weights = got[:, : 2 * cols], got[:, above:]
    back = got[:, 2 * cols : 2 * cols + by_lane]
    inputs = inputs.reshape(blocks, 2, cols, block)
    weights = weights.reshape(blocks, 2, lanes, cols, wide)
    part = dot("zikr,zijkh->jrh", inputs, weights).astype(BF16)
    back = two(jnp.sum(back.astype(F32), axis=0))

    rows = part.reshape(lanes, lanes, mine, wide).transpose(1, 0, 2, 3)
    rows = rows.reshape(lanes, lanes * mine, wide)
    got = exchange(jnp.concatenate([part, rows, to_all(back, lanes)], axis=1), LANE)
    sends, rows, own_logits = pl.pallas_call(
        middle,
        in_specs=[whole, away],
        scratch_shapes=[pltpu.VMEM((2, cls, hid), BF16), pltpu.SemaphoreType.DMA],
        out_shape=(
            jax.ShapeDtypeStruct((blocks, 4 * by_z, block), BF16),
            jax.ShapeDtypeStruct((mine, hid), BF16),
            jax.ShapeDtypeStruct((mine, cls), F32),
        ),
        compiler_params=wide_limit,
    )(got, w_two.transpose(0, 2, 1))
    got = exchange(sends, "z")
    grad = pl.pallas_call(
        sum_z,
        out_shape=jax.ShapeDtypeStruct((nodes, by_z, wide), F32),
        compiler_params=limit,
    )(got)
    grad = pl.pallas_call(
        sum_nodes,
        out_shape=jax.ShapeDtypeStruct((blocks, by_z, wide), BF16),
        compiler_params=limit,
    )(exchange(grad, "node"))

    logits, own_logits = pl.pallas_call(
        partial_logits,
        out_shape=(
            jax.ShapeDtypeStruct((lanes, 2 * mine, block), BF16),
            jax.ShapeDtypeStruct((mine, cls), F32),
        ),
        compiler_params=limit,
    )(got, near, own_logits)

    got = pl.pallas_call(
        last,
        out_shape=jax.ShapeDtypeStruct((lanes, kept + 2 * mine, block), BF16),
        compiler_params=limit,
    )(exchange(grad, "z"), logits)
    got = exchange(got, LANE)
    logits, grad = pl.pallas_call(
        finish,
        out_shape=(
            jax.ShapeDtypeStruct((mine, cls), F32),
            jax.ShapeDtypeStruct((cls, hid), F32),
        ),
        compiler_params=limit,
    )(got, own_logits)
    return rows, logits, grad.T


def solution(mesh):
    nodes = mesh.devices.shape[1]
    fine = Mesh(mesh.devices.reshape(4, 12, 2, nodes), ("x", "z", "c", "node"))
    col = ("x", "z", "c")
    rows = ("node", *col)
    in_specs = (
        P(col, "node"),
        P(None, col, None),
        P("node", None, None, None),
        P("node", None),
        P(rows, None, None),
        P("node", None),
        P(),
        P(rows, None),
    )
    out_specs = (P(rows, None), P(rows, None), P())
    return jax.shard_map(
        per_device, mesh=fine, in_specs=in_specs, out_specs=out_specs, check_vma=False
    )
```

```python
import functools

import jax
import jax.numpy as jnp
from jax import lax
from jax.experimental import pallas as pl
from jax.experimental.pallas import tpu as pltpu
from jax.sharding import Mesh, PartitionSpec as P

F32, BF16 = jnp.float32, jnp.bfloat16
LANE = ("x", "c")


def exchange(parts, axis):
    return lax.all_to_all(parts, axis, 0, 0, tiled=True)


def to_all(part, size):
    return jnp.broadcast_to(part[None], (size, *part.shape))


def dot(spec, a, b):
    return jnp.einsum(spec, a, b, preferred_element_type=F32)


def two(a):
    high = a.astype(BF16)
    return jnp.concatenate([high, (a - high.astype(F32)).astype(BF16)], axis=-2)


def near_rows(edges_in, cot_in, sends, edges, cot, sems):
    copies = [
        pltpu.make_async_copy(edges_in, edges, sems.at[0]),
        pltpu.make_async_copy(cot_in, cot, sems.at[1]),
    ]
    for copy in copies:
        copy.start()
    for copy in copies:
        copy.wait()
    rows, block = edges.shape
    mine, cls = cot.shape
    rest = jnp.concatenate([cot[:, block:], jnp.zeros((mine, 2 * block - cls), BF16)], axis=1)
    for j in range(sends.shape[0]):
        sends[j, :rows] = edges[...]
        sends[j, rows : rows + mine] = cot[:, :block]
        sends[j, rows + mine :] = rest


def pick_blocks(lists, tiles_in, w_in, chosen, own, w, tiles, sems):
    copies = [
        pltpu.make_async_copy(tiles_in, tiles, sems.at[0]),
        pltpu.make_async_copy(w_in, w, sems.at[1]),
    ]
    for copy in copies:
        copy.start()
    for copy in copies:
        copy.wait()
    fanout, blocks = lists.shape
    block = chosen.shape[2]
    own[...] = tiles[:, : blocks * block]
    for b in range(blocks):
        for k in range(fanout):
            at = pl.multiple_of(lists[k, b] * block, block)
            chosen[b * fanout + k] = tiles[:, pl.ds(at, block)]


def first(xs, by_lane, lists, got, agg, own, w, sends, edges_out):
    lanes, _, block = got.shape
    blocks, cols = agg.shape[:2]
    listed = lists.shape[0]
    mids = blocks // xs
    strips = blocks // mids
    strip = block // strips
    mine = block // lanes
    my_x, my_mid = lax.axis_index("x"), lax.axis_index("z") // strips
    my_lane = my_x * (lanes // xs) + lax.axis_index("c")
    edges = mine * listed
    total = lanes * edges
    over = (((1,), (1,)), ((), ()))
    cot = [got[:, edges : edges + mine], got[:, edges + mine :]]
    cot = jnp.concatenate([c.reshape(block, block) for c in cot], axis=1)
    shape = (by_lane, 2 * block)
    at = lax.broadcasted_iota(jnp.int32, shape, 1) - lax.broadcasted_iota(jnp.int32, shape, 0)
    pick = jnp.where(at == my_lane * by_lane, 1.0, 0.0).astype(BF16)
    cot = lax.dot_general(pick, cot, over, preferred_element_type=F32).astype(BF16)
    row = lax.broadcasted_iota(jnp.int32, (block, total), 0)
    at = lax.broadcasted_iota(jnp.int32, (block, total), 1)
    fits = at // listed == row
    spread = jnp.where(fits, 1.0, 0.0).astype(BF16)
    cot = jnp.dot(cot, spread, preferred_element_type=F32)
    at = lax.broadcasted_iota(jnp.int32, (8, total), 1)
    to = jnp.full((8, total), -1, jnp.int32)
    for x in range(xs):
        for k in range(listed):
            here = (at // (total // xs) == x) & (at % listed == k)
            to = jnp.where(here, lists[k, x * mids + my_mid], to)
    to = jnp.concatenate([to] * (block // 8), axis=0)
    back = [jnp.where(to[:by_lane] == b, cot, 0.0).astype(BF16) for b in range(blocks)]
    near = got[:, :edges].reshape(total, block)
    back = [jnp.dot(b, near, preferred_element_type=F32) for b in back]
    for mid in range(mids):
        take = jnp.where(fits & (to == my_x * mids + mid), 1.0, 0.0).astype(BF16)
        take = jnp.dot(take, near, preferred_element_type=F32).astype(BF16)
        edges_out[:, mid * block : (mid + 1) * block] = take
    pad = jnp.zeros((sends.shape[1] - block - 2 * cols - by_lane, block), F32)
    parts = []
    for b in range(blocks):
        mine_b = own[:, b * block : (b + 1) * block].astype(F32)
        parts.append(jnp.concatenate([agg[b].astype(F32), mine_b, back[b], pad], axis=0))
    high = parts[0].shape[0]
    parts = [
        jnp.concatenate(parts[x * mids : (x + 1) * mids], axis=0).astype(BF16) for x in range(xs)
    ]
    parts = jnp.concatenate(parts, axis=1)
    row = lax.broadcasted_iota(jnp.int32, (xs * block, block), 0)
    to = lax.broadcasted_iota(jnp.int32, (xs * block, block), 1)
    fits = (to // strip == row // block) & (to % strip == row % strip)
    for low in range(strips):
        move = jnp.where(fits & (row % block // strip == low), 1.0, 0.0).astype(BF16)
        moved = jnp.dot(parts, move, preferred_element_type=F32).astype(BF16)
        for mid in range(mids):
            sends[mid * strips + low, :high] = moved[mid * high : (mid + 1) * high]
    wide = w.shape[2] // lanes
    w = [w[i, :, j * wide : (j + 1) * wide].astype(F32) for i in range(2) for j in range(lanes)]
    w = jnp.concatenate(w, axis=0).astype(BF16)
    for z in range(blocks):
        sends[z, high:] = w


def sum_nodes(got, sends):
    total = got[0]
    for n in range(1, got.shape[0]):
        total = total + got[n]
    for z in range(sends.shape[0]):
        sends[z] = total.astype(BF16)


def middle(got, w_in, sends, rows, logits, w, sem):
    copy = pltpu.make_async_copy(w_in, w, sem)
    copy.start()
    lanes, wide = got.shape[0], got.shape[2]
    blocks, by_z = sends.shape[0], sends.shape[1] // 4
    block, mine = got.shape[2], rows.shape[0]
    pre = got[0, : 2 * block].astype(F32)
    for j in range(1, lanes):
        pre = pre + got[j, : 2 * block].astype(F32)
    hidden = jnp.maximum(pre, 0.0).astype(BF16)
    for j in range(lanes):
        rows[:, j * wide : (j + 1) * wide] = hidden[block + j * mine : block + (j + 1) * mine]
    hidden = hidden[:block]
    back = got[:, 2 * block :].astype(F32)
    half = back.shape[1] // 2
    back = (back[:, :half] + back[:, half:]).reshape(lanes * half, block)
    high = back.astype(BF16)
    low = (back - high.astype(F32)).astype(BF16)
    grad = jnp.dot(high, hidden, preferred_element_type=F32)
    grad = grad + jnp.dot(low, hidden, preferred_element_type=F32)
    grad = grad.reshape(blocks, by_z, wide)
    high = grad.astype(BF16)
    sends[:, :by_z] = high
    sends[:, by_z : 2 * by_z] = (grad - high.astype(F32)).astype(BF16)
    over = (((1,), (1,)), ((), ()))
    copy.wait()
    product = lax.dot_general(rows[...], w[0], over, preferred_element_type=F32)
    logits[...] = lax.dot_general(rows[...], w[1], over, preferred_element_type=F32)
    pad = jnp.zeros((mine, 2 * block - product.shape[1]), F32)
    product = jnp.concatenate([product, pad], axis=1).astype(BF16)
    for z in range(blocks):
        sends[z, 2 * by_z : 2 * by_z + mine] = product[:, :block]
        sends[z, 2 * by_z + mine :] = product[:, block:]


def sum_z(got, sends):
    by_z = sends.shape[1]
    total = got[0, : 2 * by_z].astype(F32)
    for z in range(1, got.shape[0]):
        total = total + got[z, : 2 * by_z].astype(F32)
    total = total[:by_z] + total[by_z:]
    for n in range(sends.shape[0]):
        sends[n] = total


def partial_logits(got, near, own_in, sends, own):
    lanes, block = sends.shape[0], sends.shape[2]
    mine = sends.shape[1] // 2
    cores = near.shape[1] // (got.shape[0] * mine)
    above = got.shape[1] - 2 * mine
    my_c = lax.axis_index("c")
    own[...] = own_in[...]
    rows = []
    for z in range(got.shape[0]):
        product = jnp.concatenate([got[z, above : above + mine], got[z, above + mine :]], axis=1)
        for c in range(cores):
            rows.append(jnp.where(my_c == c, product, jnp.zeros_like(product)))
    rows = jnp.concatenate(rows, axis=0)
    part = jnp.dot(near[...], rows, preferred_element_type=F32).astype(BF16)
    for j in range(lanes):
        sends[j, :mine] = part[j * mine : (j + 1) * mine, :block]
        sends[j, mine:] = part[j * mine : (j + 1) * mine, block:]


def last(grad, logits, sends):
    kept = sends.shape[1] - logits.shape[1]
    by_z = grad.shape[1]
    for j in range(sends.shape[0]):
        for z in range(kept // by_z):
            sends[j, z * by_z : (z + 1) * by_z] = grad[z]
        sends[j, kept:] = logits[j]


def finish(got, own, logits, grad):
    lanes, wide = got.shape[0], got.shape[2]
    mine, cls = logits.shape
    kept = got.shape[1] - 2 * mine
    part = got[0, kept:].astype(F32)
    for j in range(1, lanes):
        part = part + got[j, kept:].astype(F32)
    part = jnp.concatenate([part[:mine], part[mine:]], axis=1)
    logits[...] = part[:, :cls] + own[...]
    for j in range(lanes):
        grad[:, j * wide : (j + 1) * wide] = got[j, :kept].astype(F32)[:cls]


def per_device(features, w_one, adj_one, list_one, adj_two, list_two, w_two, cotangent):
    cols, sources = features.shape
    blocks, fanout = list_one.shape
    block = adj_one.shape[-1]
    mine, listed = adj_two.shape[:2]
    hid, cls = w_two.shape[1:]
    nodes = lax.axis_size("node")
    xs, cores = lax.axis_size("x"), lax.axis_size("c")
    lanes = xs * cores
    wide = hid // lanes
    by_lane = -(-cls // (8 * lanes)) * 8
    every = by_lane * lanes
    by_z = every // blocks
    kept = -(-cls // 8) * 8
    strip = mine * cores
    strips = block // strip
    mids = blocks // xs
    limit = pltpu.CompilerParams(vmem_limit_bytes=16 * 2**20)
    wide_limit = pltpu.CompilerParams(vmem_limit_bytes=60 * 2**20)
    away = pl.BlockSpec(memory_space=pltpu.HBM)
    whole = pl.BlockSpec(memory_space=pltpu.VMEM)
    scalars = pl.BlockSpec(memory_space=pltpu.SMEM)
    got = pl.pallas_call(
        near_rows,
        in_specs=[away, away],
        out_shape=jax.ShapeDtypeStruct((lanes, mine * (listed + 2), block), BF16),
        scratch_shapes=[
            pltpu.VMEM((mine * listed, block), BF16),
            pltpu.VMEM((mine, cls), BF16),
            pltpu.SemaphoreType.DMA((2,)),
        ],
        compiler_params=wide_limit,
    )(adj_two.reshape(mine * listed, block), cotangent)
    near = exchange(got, LANE)

    chosen, own, w = pl.pallas_call(
        pick_blocks,
        in_specs=[scalars, away, away],
        out_shape=(
            jax.ShapeDtypeStruct((blocks * fanout, cols, block), BF16),
            jax.ShapeDtypeStruct((cols, blocks * block), BF16),
            jax.ShapeDtypeStruct(w_one.shape, BF16),
        ),
        scratch_shapes=[pltpu.VMEM((cols, sources), BF16), pltpu.SemaphoreType.DMA((2,))],
        compiler_params=limit,
    )(list_one.T, features, w_one)
    chosen = chosen.reshape(blocks, fanout, cols, block)
    agg = dot("hkfs,hkts->hft", chosen, adj_one).astype(BF16)
    above = -(-(2 * cols + by_lane) // 16) * 16
    got, near = pl.pallas_call(
        functools.partial(first, xs, by_lane),
        in_specs=[scalars, whole, whole, whole, whole],
        out_specs=(whole, whole),
        out_shape=(
            jax.ShapeDtypeStruct((blocks, above + 2 * cols * lanes, block), BF16),
            jax.ShapeDtypeStruct((block, mids * block), BF16),
        ),
        compiler_params=limit,
    )(list_two.T, near, agg, own, w)
    got = exchange(got, "z")
    inputs, weights = got[:, : 2 * cols], got[:, above:]
    back = got[:, 2 * cols : 2 * cols + by_lane]
    inputs = inputs.reshape(blocks, 2, cols, block)
    weights = weights.reshape(blocks, 2, lanes, cols, wide)
    part = dot("zikr,zijkh->jrh", inputs, weights).astype(BF16)
    back = two(jnp.sum(back.astype(F32), axis=0))

    rows = part.reshape(lanes, lanes, mine, wide).transpose(1, 0, 2, 3)
    rows = rows.reshape(lanes, lanes * mine, wide)
    got = exchange(jnp.concatenate([part, rows, to_all(back, lanes)], axis=1), LANE)
    sends, rows, own_logits = pl.pallas_call(
        middle,
        in_specs=[whole, away],
        scratch_shapes=[pltpu.VMEM((2, cls, hid), BF16), pltpu.SemaphoreType.DMA],
        out_shape=(
            jax.ShapeDtypeStruct((blocks, 4 * by_z, block), BF16),
            jax.ShapeDtypeStruct((mine, hid), BF16),
            jax.ShapeDtypeStruct((mine, cls), F32),
        ),
        compiler_params=wide_limit,
    )(got, w_two.transpose(0, 2, 1))
    got = exchange(sends, "z")
    grad = pl.pallas_call(
        sum_z,
        out_shape=jax.ShapeDtypeStruct((nodes, by_z, wide), F32),
        compiler_params=limit,
    )(got)
    grad = pl.pallas_call(
        sum_nodes,
        out_shape=jax.ShapeDtypeStruct((blocks, by_z, wide), BF16),
        compiler_params=limit,
    )(exchange(grad, "node"))

    logits, own_logits = pl.pallas_call(
        partial_logits,
        out_shape=(
            jax.ShapeDtypeStruct((lanes, 2 * mine, block), BF16),
            jax.ShapeDtypeStruct((mine, cls), F32),
        ),
        compiler_params=limit,
    )(got, near, own_logits)

    got = pl.pallas_call(
        last,
        out_shape=jax.ShapeDtypeStruct((lanes, kept + 2 * mine, block), BF16),
        compiler_params=limit,
    )(exchange(grad, "z"), logits)
    got = exchange(got, LANE)
    logits, grad = pl.pallas_call(
        finish,
        out_shape=(
            jax.ShapeDtypeStruct((mine, cls), F32),
            jax.ShapeDtypeStruct((cls, hid), F32),
        ),
        compiler_params=limit,
    )(got, own_logits)
    return rows, logits, grad.T


def solution(mesh):
    nodes = mesh.devices.shape[1]
    fine = Mesh(mesh.devices.reshape(4, 12, 2, nodes), ("x", "z", "c", "node"))
    col = ("x", "z", "c")
    rows = ("node", *col)
    in_specs = (
        P(col, "node"),
        P(None, col, None),
        P("node", None, None, None),
        P("node", None),
        P(rows, None, None),
        P("node", None),
        P(),
        P(rows, None),
    )
    out_specs = (P(rows, None), P(rows, None), P())
    return jax.shard_map(
        per_device, mesh=fine, in_specs=in_specs, out_specs=out_specs, check_vma=False
    )
```

```python
import functools

import jax
import jax.numpy as jnp
from jax import lax
from jax.experimental import pallas as pl
from jax.experimental.pallas import tpu as pltpu
from jax.sharding import Mesh, PartitionSpec as P

F32, BF16 = jnp.float32, jnp.bfloat16
LANE = ("x", "c")


def exchange(parts, axis):
    return lax.all_to_all(parts, axis, 0, 0, tiled=True)


def to_all(part, size):
    return jnp.broadcast_to(part[None], (size, *part.shape))


def dot(spec, a, b):
    return jnp.einsum(spec, a, b, preferred_element_type=F32)


def two(a):
    high = a.astype(BF16)
    return jnp.concatenate([high, (a - high.astype(F32)).astype(BF16)], axis=-2)


def near_rows(edges_in, cot_in, sends, edges, cot, sems):
    copies = [
        pltpu.make_async_copy(edges_in, edges, sems.at[0]),
        pltpu.make_async_copy(cot_in, cot, sems.at[1]),
    ]
    for copy in copies:
        copy.start()
    for copy in copies:
        copy.wait()
    rows, block = edges.shape
    mine, cls = cot.shape
    rest = jnp.concatenate([cot[:, block:], jnp.zeros((mine, 2 * block - cls), BF16)], axis=1)
    for j in range(sends.shape[0]):
        sends[j, :rows] = edges[...]
        sends[j, rows : rows + mine] = cot[:, :block]
        sends[j, rows + mine :] = rest


def pick_blocks(lists, tiles_in, w_in, chosen, own, w, tiles, sems):
    copies = [
        pltpu.make_async_copy(tiles_in, tiles, sems.at[0]),
        pltpu.make_async_copy(w_in, w, sems.at[1]),
    ]
    for copy in copies:
        copy.start()
    for copy in copies:
        copy.wait()
    fanout, blocks = lists.shape
    block = chosen.shape[2]
    own[...] = tiles[:, : blocks * block]
    for b in range(blocks):
        for k in range(fanout):
            at = pl.multiple_of(lists[k, b] * block, block)
            chosen[b * fanout + k] = tiles[:, pl.ds(at, block)]


def first(xs, by_lane, lists, got, agg, own, w, sends, edges_out):
    lanes, _, block = got.shape
    blocks, cols = agg.shape[:2]
    listed = lists.shape[0]
    mids = blocks // xs
    strips = blocks // mids
    strip = block // strips
    mine = block // lanes
    my_x, my_mid = lax.axis_index("x"), lax.axis_index("z") // strips
    my_lane = my_x * (lanes // xs) + lax.axis_index("c")
    edges = mine * listed
    total = lanes * edges
    over = (((1,), (1,)), ((), ()))
    cot = [got[:, edges : edges + mine], got[:, edges + mine :]]
    cot = jnp.concatenate([c.reshape(block, block) for c in cot], axis=1)
    shape = (by_lane, 2 * block)
    at = lax.broadcasted_iota(jnp.int32, shape, 1) - lax.broadcasted_iota(jnp.int32, shape, 0)
    pick = jnp.where(at == my_lane * by_lane, 1.0, 0.0).astype(BF16)
    cot = lax.dot_general(pick, cot, over, preferred_element_type=F32).astype(BF16)
    row = lax.broadcasted_iota(jnp.int32, (block, total), 0)
    at = lax.broadcasted_iota(jnp.int32, (block, total), 1)
    fits = at // listed == row
    spread = jnp.where(fits, 1.0, 0.0).astype(BF16)
    cot = jnp.dot(cot, spread, preferred_element_type=F32)
    at = lax.broadcasted_iota(jnp.int32, (8, total), 1)
    to = jnp.full((8, total), -1, jnp.int32)
    for x in range(xs):
        for k in range(listed):
            here = (at // (total // xs) == x) & (at % listed == k)
            to = jnp.where(here, lists[k, x * mids + my_mid], to)
    to = jnp.concatenate([to] * (block // 8), axis=0)
    back = [jnp.where(to[:by_lane] == b, cot, 0.0).astype(BF16) for b in range(blocks)]
    near = got[:, :edges].reshape(total, block)
    back = [jnp.dot(b, near, preferred_element_type=F32) for b in back]
    for mid in range(mids):
        take = jnp.where(fits & (to == my_x * mids + mid), 1.0, 0.0).astype(BF16)
        take = jnp.dot(take, near, preferred_element_type=F32).astype(BF16)
        edges_out[:, mid * block : (mid + 1) * block] = take
    pad = jnp.zeros((-(2 * cols + by_lane) % 16, block), F32)
    parts = []
    for b in range(blocks):
        mine_b = own[:, b * block : (b + 1) * block].astype(F32)
        parts.append(jnp.concatenate([agg[b].astype(F32), mine_b, back[b], pad], axis=0))
    high = parts[0].shape[0]
    parts = [
        jnp.concatenate(parts[x * mids : (x + 1) * mids], axis=0).astype(BF16) for x in range(xs)
    ]
    parts = jnp.concatenate(parts, axis=1)
    row = lax.broadcasted_iota(jnp.int32, (xs * block, block), 0)
    to = lax.broadcasted_iota(jnp.int32, (xs * block, block), 1)
    fits = (to // strip == row // block) & (to % strip == row % strip)
    for low in range(strips):
        move = jnp.where(fits & (row % block // strip == low), 1.0, 0.0).astype(BF16)
        moved = jnp.dot(parts, move, preferred_element_type=F32).astype(BF16)
        for mid in range(mids):
            at = mid * high + 2 * cols
            sends[mid * strips + low, : 2 * cols] = moved[mid * high : at]
            sends[mid * strips + low, 2 * cols + block :] = moved[at : at + by_lane]
    wide = w.shape[2] // lanes
    w = [w[i, :, j * wide : (j + 1) * wide].astype(F32) for i in range(2) for j in range(lanes)]
    w = jnp.concatenate(w, axis=0).astype(BF16)
    for z in range(blocks):
        sends[z, 2 * cols : 2 * cols + block] = w


def sum_nodes(got, sends):
    total = got[0]
    for n in range(1, got.shape[0]):
        total = total + got[n]
    for z in range(sends.shape[0]):
        sends[z] = total.astype(BF16)


def middle(got, w_in, sends, rows, logits, w, sem):
    copy = pltpu.make_async_copy(w_in, w, sem)
    copy.start()
    lanes, wide = got.shape[0], got.shape[2]
    blocks, block, mine = sends.shape[0], got.shape[2], rows.shape[0]
    by_z = (got.shape[1] - 2 * block) // 2 * lanes // blocks
    pre = got[0, : 2 * block].astype(F32)
    for j in range(1, lanes):
        pre = pre + got[j, : 2 * block].astype(F32)
    hidden = jnp.maximum(pre, 0.0).astype(BF16)
    for j in range(lanes):
        rows[:, j * wide : (j + 1) * wide] = hidden[block + j * mine : block + (j + 1) * mine]
    hidden = hidden[:block]
    back = got[:, 2 * block :].astype(F32)
    half = back.shape[1] // 2
    back = (back[:, :half] + back[:, half:]).reshape(lanes * half, block)
    high = back.astype(BF16)
    low = (back - high.astype(F32)).astype(BF16)
    grad = jnp.dot(high, hidden, preferred_element_type=F32)
    grad = grad + jnp.dot(low, hidden, preferred_element_type=F32)
    grad = grad.reshape(blocks, by_z, wide)
    high = grad.astype(BF16)
    sends[:, :by_z] = high
    sends[:, by_z : 2 * by_z] = (grad - high.astype(F32)).astype(BF16)
    over = (((1,), (1,)), ((), ()))
    copy.wait()
    product = lax.dot_general(rows[...], w[0], over, preferred_element_type=F32)
    logits[...] = lax.dot_general(rows[...], w[1], over, preferred_element_type=F32)
    pad = jnp.zeros((mine, 2 * block - product.shape[1]), F32)
    product = jnp.concatenate([product, pad], axis=1)
    rest = product[:, block : block + block // 2]
    rest = jnp.concatenate([rest[: mine // 2], rest[mine // 2 :]], axis=1).astype(BF16)
    product = product[:, :block].astype(BF16)
    for z in range(blocks):
        sends[z, 2 * by_z : 2 * by_z + mine] = product
        sends[z, 2 * by_z + mine :] = rest


def sum_z(got, sends):
    by_z = sends.shape[1]
    total = got[0, : 2 * by_z].astype(F32)
    for z in range(1, got.shape[0]):
        total = total + got[z, : 2 * by_z].astype(F32)
    total = total[:by_z] + total[by_z:]
    for n in range(sends.shape[0]):
        sends[n] = total


def partial_logits(got, near, own_in, sends, own):
    lanes, block = sends.shape[0], sends.shape[2]
    mine = sends.shape[1] // 2
    cores = near.shape[1] // (got.shape[0] * mine)
    above = got.shape[1] - mine - mine // 2
    none = jnp.zeros((mine, block // 2), F32)
    my_c = lax.axis_index("c")
    own[...] = own_in[...]
    rows = []
    for z in range(got.shape[0]):
        rest = got[z, above + mine :].astype(F32)
        rest = jnp.concatenate([rest[:, : block // 2], rest[:, block // 2 :]], axis=0)
        rest = jnp.concatenate([rest, none], axis=1).astype(BF16)
        product = jnp.concatenate([got[z, above : above + mine], rest], axis=1)
        for c in range(cores):
            rows.append(jnp.where(my_c == c, product, jnp.zeros_like(product)))
    rows = jnp.concatenate(rows, axis=0)
    part = jnp.dot(near[...], rows, preferred_element_type=F32).astype(BF16)
    for j in range(lanes):
        sends[j, :mine] = part[j * mine : (j + 1) * mine, :block]
        sends[j, mine:] = part[j * mine : (j + 1) * mine, block:]


def last(grad, logits, sends):
    kept = sends.shape[1] - logits.shape[1]
    by_z = grad.shape[1]
    for j in range(sends.shape[0]):
        for z in range(kept // by_z):
            sends[j, z * by_z : (z + 1) * by_z] = grad[z]
        sends[j, kept:] = logits[j]


def finish(got, own, logits, grad):
    lanes, wide = got.shape[0], got.shape[2]
    mine, cls = logits.shape
    kept = got.shape[1] - 2 * mine
    part = got[0, kept:].astype(F32)
    for j in range(1, lanes):
        part = part + got[j, kept:].astype(F32)
    part = jnp.concatenate([part[:mine], part[mine:]], axis=1)
    logits[...] = part[:, :cls] + own[...]
    for j in range(lanes):
        grad[:, j * wide : (j + 1) * wide] = got[j, :kept].astype(F32)[:cls]


def per_device(features, w_one, adj_one, list_one, adj_two, list_two, w_two, cotangent):
    cols, sources = features.shape
    blocks, fanout = list_one.shape
    block = adj_one.shape[-1]
    mine, listed = adj_two.shape[:2]
    hid, cls = w_two.shape[1:]
    nodes = lax.axis_size("node")
    xs, cores = lax.axis_size("x"), lax.axis_size("c")
    lanes = xs * cores
    wide = hid // lanes
    by_lane = -(-cls // (8 * lanes)) * 8
    every = by_lane * lanes
    by_z = every // blocks
    kept = -(-cls // 8) * 8
    strip = mine * cores
    strips = block // strip
    mids = blocks // xs
    limit = pltpu.CompilerParams(vmem_limit_bytes=16 * 2**20)
    wide_limit = pltpu.CompilerParams(vmem_limit_bytes=60 * 2**20)
    away = pl.BlockSpec(memory_space=pltpu.HBM)
    whole = pl.BlockSpec(memory_space=pltpu.VMEM)
    scalars = pl.BlockSpec(memory_space=pltpu.SMEM)
    got = pl.pallas_call(
        near_rows,
        in_specs=[away, away],
        out_shape=jax.ShapeDtypeStruct((lanes, mine * (listed + 2), block), BF16),
        scratch_shapes=[
            pltpu.VMEM((mine * listed, block), BF16),
            pltpu.VMEM((mine, cls), BF16),
            pltpu.SemaphoreType.DMA((2,)),
        ],
        compiler_params=wide_limit,
    )(adj_two.reshape(mine * listed, block), cotangent)
    near = exchange(got, LANE)

    chosen, own, w = pl.pallas_call(
        pick_blocks,
        in_specs=[scalars, away, away],
        out_shape=(
            jax.ShapeDtypeStruct((blocks * fanout, cols, block), BF16),
            jax.ShapeDtypeStruct((cols, blocks * block), BF16),
            jax.ShapeDtypeStruct(w_one.shape, BF16),
        ),
        scratch_shapes=[pltpu.VMEM((cols, sources), BF16), pltpu.SemaphoreType.DMA((2,))],
        compiler_params=limit,
    )(list_one.T, features, w_one)
    chosen = chosen.reshape(blocks, fanout, cols, block)
    agg = dot("hkfs,hkts->hft", chosen, adj_one).astype(BF16)
    above = 2 * cols + 2 * cols * lanes
    got, near = pl.pallas_call(
        functools.partial(first, xs, by_lane),
        in_specs=[scalars, whole, whole, whole, whole],
        out_specs=(whole, whole),
        out_shape=(
            jax.ShapeDtypeStruct((blocks, above + by_lane, block), BF16),
            jax.ShapeDtypeStruct((block, mids * block), BF16),
        ),
        compiler_params=limit,
    )(list_two.T, near, agg, own, w)
    got = exchange(got, "z")
    inputs, weights, back = jnp.split(got, (2 * cols, above), axis=1)
    inputs = inputs.reshape(blocks, 2, cols, block)
    weights = weights.reshape(blocks, 2, lanes, cols, wide)
    part = dot("zikr,zijkh->jrh", inputs, weights).astype(BF16)
    back = two(jnp.sum(back.astype(F32), axis=0))

    rows = part.reshape(lanes, lanes, mine, wide).transpose(1, 0, 2, 3)
    rows = rows.reshape(lanes, lanes * mine, wide)
    got = exchange(jnp.concatenate([part, rows, to_all(back, lanes)], axis=1), LANE)
    sends, rows, own_logits = pl.pallas_call(
        middle,
        in_specs=[whole, away],
        scratch_shapes=[pltpu.VMEM((2, cls, hid), BF16), pltpu.SemaphoreType.DMA],
        out_shape=(
            jax.ShapeDtypeStruct((blocks, 2 * by_z + mine + mine // 2, block), BF16),
            jax.ShapeDtypeStruct((mine, hid), BF16),
            jax.ShapeDtypeStruct((mine, cls), F32),
        ),
        compiler_params=wide_limit,
    )(got, w_two.transpose(0, 2, 1))
    got = exchange(sends, "z")
    grad = pl.pallas_call(
        sum_z,
        out_shape=jax.ShapeDtypeStruct((nodes, by_z, wide), F32),
        compiler_params=limit,
    )(got)
    grad = pl.pallas_call(
        sum_nodes,
        out_shape=jax.ShapeDtypeStruct((blocks, by_z, wide), BF16),
        compiler_params=limit,
    )(exchange(grad, "node"))

    logits, own_logits = pl.pallas_call(
        partial_logits,
        out_shape=(
            jax.ShapeDtypeStruct((lanes, 2 * mine, block), BF16),
            jax.ShapeDtypeStruct((mine, cls), F32),
        ),
        compiler_params=limit,
    )(got, near, own_logits)

    got = pl.pallas_call(
        last,
        out_shape=jax.ShapeDtypeStruct((lanes, kept + 2 * mine, block), BF16),
        compiler_params=limit,
    )(exchange(grad, "z"), logits)
    got = exchange(got, LANE)
    logits, grad = pl.pallas_call(
        finish,
        out_shape=(
            jax.ShapeDtypeStruct((mine, cls), F32),
            jax.ShapeDtypeStruct((cls, hid), F32),
        ),
        compiler_params=limit,
    )(got, own_logits)
    return rows, logits, grad.T


def solution(mesh):
    nodes = mesh.devices.shape[1]
    fine = Mesh(mesh.devices.reshape(4, 12, 2, nodes), ("x", "z", "c", "node"))
    col = ("x", "z", "c")
    rows = ("node", *col)
    in_specs = (
        P(col, "node"),
        P(None, col, None),
        P("node", None, None, None),
        P("node", None),
        P(rows, None, None),
        P("node", None),
        P(),
        P(rows, None),
    )
    out_specs = (P(rows, None), P(rows, None), P())
    return jax.shard_map(
        per_device, mesh=fine, in_specs=in_specs, out_specs=out_specs, check_vma=False
    )
```

```python
import functools

import jax
import jax.numpy as jnp
from jax import lax
from jax.experimental import pallas as pl
from jax.experimental.pallas import tpu as pltpu
from jax.sharding import Mesh, PartitionSpec as P

F32, BF16 = jnp.float32, jnp.bfloat16
LANE = ("x", "c")


def exchange(parts, axis):
    return lax.all_to_all(parts, axis, 0, 0, tiled=True)


def to_all(part, size):
    return jnp.broadcast_to(part[None], (size, *part.shape))


def dot(spec, a, b):
    return jnp.einsum(spec, a, b, preferred_element_type=F32)


def two(a):
    high = a.astype(BF16)
    return jnp.concatenate([high, (a - high.astype(F32)).astype(BF16)], axis=-2)


def near_rows(edges_in, cot_in, sends, edges, cot, sems):
    copies = [
        pltpu.make_async_copy(edges_in, edges, sems.at[0]),
        pltpu.make_async_copy(cot_in, cot, sems.at[1]),
    ]
    for copy in copies:
        copy.start()
    for copy in copies:
        copy.wait()
    rows, block = edges.shape
    mine, cls = cot.shape
    rest = jnp.concatenate([cot[:, block:], jnp.zeros((mine, 2 * block - cls), BF16)], axis=1)
    for j in range(sends.shape[0]):
        sends[j, :rows] = edges[...]
        sends[j, rows : rows + mine] = cot[:, :block]
        sends[j, rows + mine :] = rest


def pick_blocks(lists, tiles_in, w_in, chosen, own, w, tiles, sems):
    copies = [
        pltpu.make_async_copy(tiles_in, tiles, sems.at[0]),
        pltpu.make_async_copy(w_in, w, sems.at[1]),
    ]
    for copy in copies:
        copy.start()
    for copy in copies:
        copy.wait()
    fanout, blocks = lists.shape
    block = chosen.shape[2]
    own[...] = tiles[:, : blocks * block]
    for b in range(blocks):
        for k in range(fanout):
            at = pl.multiple_of(lists[k, b] * block, block)
            chosen[b * fanout + k] = tiles[:, pl.ds(at, block)]


def first(xs, by_lane, lists, got, agg, own, w, sends, edges_out):
    lanes, _, block = got.shape
    blocks, cols = agg.shape[:2]
    listed = lists.shape[0]
    mids = blocks // xs
    strips = blocks // mids
    strip = block // strips
    mine = block // lanes
    my_x, my_mid = lax.axis_index("x"), lax.axis_index("z") // strips
    my_lane = my_x * (lanes // xs) + lax.axis_index("c")
    edges = mine * listed
    total = lanes * edges
    over = (((1,), (1,)), ((), ()))
    cot = [got[:, edges : edges + mine], got[:, edges + mine :]]
    cot = jnp.concatenate([c.reshape(block, block) for c in cot], axis=1)
    shape = (by_lane, 2 * block)
    at = lax.broadcasted_iota(jnp.int32, shape, 1) - lax.broadcasted_iota(jnp.int32, shape, 0)
    pick = jnp.where(at == my_lane * by_lane, 1.0, 0.0).astype(BF16)
    cot = lax.dot_general(pick, cot, over, preferred_element_type=F32).astype(BF16)
    row = lax.broadcasted_iota(jnp.int32, (block, total), 0)
    at = lax.broadcasted_iota(jnp.int32, (block, total), 1)
    fits = at // listed == row
    spread = jnp.where(fits, 1.0, 0.0).astype(BF16)
    cot = jnp.dot(cot, spread, preferred_element_type=F32)
    at = lax.broadcasted_iota(jnp.int32, (8, total), 1)
    to = jnp.full((8, total), -1, jnp.int32)
    for x in range(xs):
        for k in range(listed):
            here = (at // (total // xs) == x) & (at % listed == k)
            to = jnp.where(here, lists[k, x * mids + my_mid], to)
    to = jnp.concatenate([to] * (block // 8), axis=0)
    back = [jnp.where(to[:by_lane] == b, cot, 0.0).astype(BF16) for b in range(blocks)]
    near = got[:, :edges].reshape(total, block)
    back = [jnp.dot(b, near, preferred_element_type=F32) for b in back]
    for mid in range(mids):
        take = jnp.where(fits & (to == my_x * mids + mid), 1.0, 0.0).astype(BF16)
        take = jnp.dot(take, near, preferred_element_type=F32).astype(BF16)
        edges_out[:, mid * block : (mid + 1) * block] = take
    pad = jnp.zeros((-(2 * cols + by_lane) % 16, block), F32)
    parts = []
    for b in range(blocks):
        mine_b = own[:, b * block : (b + 1) * block].astype(F32)
        parts.append(jnp.concatenate([agg[b].astype(F32), mine_b, back[b], pad], axis=0))
    high = parts[0].shape[0]
    parts = [
        jnp.concatenate(parts[x * mids : (x + 1) * mids], axis=0).astype(BF16) for x in range(xs)
    ]
    parts = jnp.concatenate(parts, axis=1)
    row = lax.broadcasted_iota(jnp.int32, (xs * block, block), 0)
    to = lax.broadcasted_iota(jnp.int32, (xs * block, block), 1)
    fits = (to // strip == row // block) & (to % strip == row % strip)
    for low in range(strips):
        move = jnp.where(fits & (row % block // strip == low), 1.0, 0.0).astype(BF16)
        moved = jnp.dot(parts, move, preferred_element_type=F32).astype(BF16)
        for mid in range(mids):
            at = mid * high + 2 * cols
            sends[mid * strips + low, : 2 * cols] = moved[mid * high : at]
            sends[mid * strips + low, 2 * cols + block :] = moved[at : at + by_lane]
    wide = w.shape[2] // lanes
    w = [w[i, :, j * wide : (j + 1) * wide].astype(F32) for i in range(2) for j in range(lanes)]
    w = jnp.concatenate(w, axis=0).astype(BF16)
    for z in range(blocks):
        sends[z, 2 * cols : 2 * cols + block] = w


def sum_nodes(got, sends):
    total = got[0]
    for n in range(1, got.shape[0]):
        total = total + got[n]
    for z in range(sends.shape[0]):
        sends[z] = total.astype(BF16)


def middle(got, w_in, sends, rows, logits, w, sem):
    copy = pltpu.make_async_copy(w_in, w, sem)
    copy.start()
    lanes, wide = got.shape[0], got.shape[2]
    blocks, block, mine = sends.shape[0], got.shape[2], rows.shape[0]
    by_z = (got.shape[1] - 2 * block) // 2 * lanes // blocks
    pre = got[0, : 2 * block].astype(F32)
    for j in range(1, lanes):
        pre = pre + got[j, : 2 * block].astype(F32)
    hidden = jnp.maximum(pre, 0.0).astype(BF16)
    for j in range(lanes):
        rows[:, j * wide : (j + 1) * wide] = hidden[block + j * mine : block + (j + 1) * mine]
    hidden = hidden[:block]
    back = got[:, 2 * block :].astype(F32)
    half = back.shape[1] // 2
    back = (back[:, :half] + back[:, half:]).reshape(lanes * half, block)
    high = back.astype(BF16)
    low = (back - high.astype(F32)).astype(BF16)
    grad = jnp.dot(high, hidden, preferred_element_type=F32)
    grad = grad + jnp.dot(low, hidden, preferred_element_type=F32)
    grad = grad.reshape(blocks, by_z, wide)
    high = grad.astype(BF16)
    sends[:, :by_z] = high
    sends[:, by_z : 2 * by_z] = (grad - high.astype(F32)).astype(BF16)
    over = (((1,), (1,)), ((), ()))
    copy.wait()
    product = lax.dot_general(rows[...], w[0], over, preferred_element_type=F32)
    logits[...] = lax.dot_general(rows[...], w[1], over, preferred_element_type=F32)
    pad = jnp.zeros((mine, 2 * block - product.shape[1]), F32)
    product = jnp.concatenate([product, pad], axis=1)
    rest = product[:, block : block + block // 2]
    rest = jnp.concatenate([rest[: mine // 2], rest[mine // 2 :]], axis=1).astype(BF16)
    product = product[:, :block].astype(BF16)
    for z in range(blocks):
        sends[z, 2 * by_z : 2 * by_z + mine] = product
        sends[z, 2 * by_z + mine :] = rest


def sum_z(got, sends):
    by_z = sends.shape[1]
    total = got[0, : 2 * by_z].astype(F32)
    for z in range(1, got.shape[0]):
        total = total + got[z, : 2 * by_z].astype(F32)
    total = total[:by_z] + total[by_z:]
    for n in range(sends.shape[0]):
        sends[n] = total


def partial_logits(got, near, own_in, sends, own):
    lanes, block = sends.shape[0], sends.shape[2]
    mine = sends.shape[1] // 2
    cores = near.shape[1] // (got.shape[0] * mine)
    above = got.shape[1] - mine - mine // 2
    none = jnp.zeros((mine, block // 2), F32)
    my_c = lax.axis_index("c")
    own[...] = own_in[...]
    rows = []
    for z in range(got.shape[0]):
        rest = got[z, above + mine :].astype(F32)
        rest = jnp.concatenate([rest[:, : block // 2], rest[:, block // 2 :]], axis=0)
        rest = jnp.concatenate([rest, none], axis=1).astype(BF16)
        product = jnp.concatenate([got[z, above : above + mine], rest], axis=1)
        for c in range(cores):
            rows.append(jnp.where(my_c == c, product, jnp.zeros_like(product)))
    rows = jnp.concatenate(rows, axis=0)
    part = jnp.dot(near[...], rows, preferred_element_type=F32).astype(BF16)
    for j in range(lanes):
        sends[j, :mine] = part[j * mine : (j + 1) * mine, :block]
        sends[j, mine:] = part[j * mine : (j + 1) * mine, block:]


def last(grad, logits, sends):
    kept = sends.shape[1] - logits.shape[1]
    by_z = grad.shape[1]
    for j in range(sends.shape[0]):
        for z in range(kept // by_z):
            sends[j, z * by_z : (z + 1) * by_z] = grad[z]
        sends[j, kept:] = logits[j]


def finish(got, own, logits, grad):
    lanes, wide = got.shape[0], got.shape[2]
    mine, cls = logits.shape
    kept = got.shape[1] - 2 * mine
    part = got[0, kept:].astype(F32)
    for j in range(1, lanes):
        part = part + got[j, kept:].astype(F32)
    part = jnp.concatenate([part[:mine], part[mine:]], axis=1)
    logits[...] = part[:, :cls] + own[...]
    for j in range(lanes):
        grad[:, j * wide : (j + 1) * wide] = got[j, :kept].astype(F32)[:cls]


def per_device(features, w_one, adj_one, list_one, adj_two, list_two, w_two, cotangent):
    cols, sources = features.shape
    blocks, fanout = list_one.shape
    block = adj_one.shape[-1]
    mine, listed = adj_two.shape[:2]
    hid, cls = w_two.shape[1:]
    nodes = lax.axis_size("node")
    xs, cores = lax.axis_size("x"), lax.axis_size("c")
    lanes = xs * cores
    wide = hid // lanes
    by_lane = -(-cls // (8 * lanes)) * 8
    every = by_lane * lanes
    by_z = every // blocks
    kept = -(-cls // 8) * 8
    strip = mine * cores
    strips = block // strip
    mids = blocks // xs
    limit = pltpu.CompilerParams(vmem_limit_bytes=16 * 2**20)
    pick_limit = pltpu.CompilerParams(vmem_limit_bytes=64 * 2**20 - 3650 * 2**10)
    wide_limit = pltpu.CompilerParams(vmem_limit_bytes=60 * 2**20)
    away = pl.BlockSpec(memory_space=pltpu.HBM)
    whole = pl.BlockSpec(memory_space=pltpu.VMEM)
    scalars = pl.BlockSpec(memory_space=pltpu.SMEM)
    got = pl.pallas_call(
        near_rows,
        in_specs=[away, away],
        out_shape=jax.ShapeDtypeStruct((lanes, mine * (listed + 2), block), BF16),
        scratch_shapes=[
            pltpu.VMEM((mine * listed, block), BF16),
            pltpu.VMEM((mine, cls), BF16),
            pltpu.SemaphoreType.DMA((2,)),
        ],
        compiler_params=wide_limit,
    )(adj_two.reshape(mine * listed, block), cotangent)
    near = exchange(got, LANE)

    chosen, own, w = pl.pallas_call(
        pick_blocks,
        in_specs=[scalars, away, away],
        out_shape=(
            jax.ShapeDtypeStruct((blocks * fanout, cols, block), BF16),
            jax.ShapeDtypeStruct((cols, blocks * block), BF16),
            jax.ShapeDtypeStruct(w_one.shape, BF16),
        ),
        scratch_shapes=[pltpu.VMEM((cols, sources), BF16), pltpu.SemaphoreType.DMA((2,))],
        compiler_params=pick_limit,
    )(list_one.T, features, w_one)
    chosen = chosen.reshape(blocks, fanout, cols, block)
    agg = dot("hkfs,hkts->hft", chosen, adj_one).astype(BF16)
    above = 2 * cols + 2 * cols * lanes
    got, near = pl.pallas_call(
        functools.partial(first, xs, by_lane),
        in_specs=[scalars, whole, whole, whole, whole],
        out_specs=(whole, whole),
        out_shape=(
            jax.ShapeDtypeStruct((blocks, above + by_lane, block), BF16),
            jax.ShapeDtypeStruct((block, mids * block), BF16),
        ),
        compiler_params=limit,
    )(list_two.T, near, agg, own, w)
    got = exchange(got, "z")
    inputs, weights, back = jnp.split(got, (2 * cols, above), axis=1)
    inputs = inputs.reshape(blocks, 2, cols, block)
    weights = weights.reshape(blocks, 2, lanes, cols, wide)
    part = dot("zikr,zijkh->jrh", inputs, weights).astype(BF16)
    back = two(jnp.sum(back.astype(F32), axis=0))

    rows = part.reshape(lanes, lanes, mine, wide).transpose(1, 0, 2, 3)
    rows = rows.reshape(lanes, lanes * mine, wide)
    got = exchange(jnp.concatenate([part, rows, to_all(back, lanes)], axis=1), LANE)
    sends, rows, own_logits = pl.pallas_call(
        middle,
        in_specs=[whole, away],
        scratch_shapes=[pltpu.VMEM((2, cls, hid), BF16), pltpu.SemaphoreType.DMA],
        out_shape=(
            jax.ShapeDtypeStruct((blocks, 2 * by_z + mine + mine // 2, block), BF16),
            jax.ShapeDtypeStruct((mine, hid), BF16),
            jax.ShapeDtypeStruct((mine, cls), F32),
        ),
        compiler_params=wide_limit,
    )(got, w_two.transpose(0, 2, 1))
    got = exchange(sends, "z")
    grad = pl.pallas_call(
        sum_z,
        out_shape=jax.ShapeDtypeStruct((nodes, by_z, wide), F32),
        compiler_params=limit,
    )(got)
    grad = pl.pallas_call(
        sum_nodes,
        out_shape=jax.ShapeDtypeStruct((blocks, by_z, wide), BF16),
        compiler_params=limit,
    )(exchange(grad, "node"))

    logits, own_logits = pl.pallas_call(
        partial_logits,
        out_shape=(
            jax.ShapeDtypeStruct((lanes, 2 * mine, block), BF16),
            jax.ShapeDtypeStruct((mine, cls), F32),
        ),
        compiler_params=limit,
    )(got, near, own_logits)

    got = pl.pallas_call(
        last,
        out_shape=jax.ShapeDtypeStruct((lanes, kept + 2 * mine, block), BF16),
        compiler_params=limit,
    )(exchange(grad, "z"), logits)
    got = exchange(got, LANE)
    logits, grad = pl.pallas_call(
        finish,
        out_shape=(
            jax.ShapeDtypeStruct((mine, cls), F32),
            jax.ShapeDtypeStruct((cls, hid), F32),
        ),
        compiler_params=limit,
    )(got, own_logits)
    return rows, logits, grad.T


def solution(mesh):
    nodes = mesh.devices.shape[1]
    fine = Mesh(mesh.devices.reshape(4, 12, 2, nodes), ("x", "z", "c", "node"))
    col = ("x", "z", "c")
    rows = ("node", *col)
    in_specs = (
        P(col, "node"),
        P(None, col, None),
        P("node", None, None, None),
        P("node", None),
        P(rows, None, None),
        P("node", None),
        P(),
        P(rows, None),
    )
    out_specs = (P(rows, None), P(rows, None), P())
    return jax.shard_map(
        per_device, mesh=fine, in_specs=in_specs, out_specs=out_specs, check_vma=False
    )
```

```python
import functools

import jax
import jax.numpy as jnp
from jax import lax
from jax.experimental import pallas as pl
from jax.experimental.pallas import tpu as pltpu
from jax.sharding import Mesh, PartitionSpec as P

F32, BF16 = jnp.float32, jnp.bfloat16
LANE = ("x", "c")


def exchange(parts, axis):
    return lax.all_to_all(parts, axis, 0, 0, tiled=True)


def to_all(part, size):
    return jnp.broadcast_to(part[None], (size, *part.shape))


def dot(spec, a, b):
    return jnp.einsum(spec, a, b, preferred_element_type=F32)


def two(a):
    high = a.astype(BF16)
    return jnp.concatenate([high, (a - high.astype(F32)).astype(BF16)], axis=-2)


def near_rows(edges_in, cot_in, sends, edges, cot, sems):
    copies = [
        pltpu.make_async_copy(edges_in, edges, sems.at[0]),
        pltpu.make_async_copy(cot_in, cot, sems.at[1]),
    ]
    for copy in copies:
        copy.start()
    for copy in copies:
        copy.wait()
    rows, block = edges.shape
    mine, cls = cot.shape
    rest = jnp.concatenate([cot[:, block:], jnp.zeros((mine, 2 * block - cls), BF16)], axis=1)
    for j in range(sends.shape[0]):
        sends[j, :rows] = edges[...]
        sends[j, rows : rows + mine] = cot[:, :block]
        sends[j, rows + mine :] = rest


def pick_blocks(lists, tiles_in, chosen, own, tiles, sem):
    copy = pltpu.make_async_copy(tiles_in, tiles, sem)
    copy.start()
    copy.wait()
    fanout, blocks = lists.shape
    block = chosen.shape[2]
    own[...] = tiles[:, : blocks * block]
    for b in range(blocks):
        for k in range(fanout):
            at = pl.multiple_of(lists[k, b] * block, block)
            chosen[b * fanout + k] = tiles[:, pl.ds(at, block)]


def first(xs, by_lane, lists, got, agg, own, w, sends, edges_out):
    lanes, _, block = got.shape
    blocks, cols = agg.shape[:2]
    listed = lists.shape[0]
    mids = blocks // xs
    strips = blocks // mids
    strip = block // strips
    mine = block // lanes
    my_x, my_mid = lax.axis_index("x"), lax.axis_index("z") // strips
    my_lane = my_x * (lanes // xs) + lax.axis_index("c")
    edges = mine * listed
    total = lanes * edges
    over = (((1,), (1,)), ((), ()))
    cot = [got[:, edges : edges + mine], got[:, edges + mine :]]
    cot = jnp.concatenate([c.reshape(block, block) for c in cot], axis=1)
    shape = (by_lane, 2 * block)
    at = lax.broadcasted_iota(jnp.int32, shape, 1) - lax.broadcasted_iota(jnp.int32, shape, 0)
    pick = jnp.where(at == my_lane * by_lane, 1.0, 0.0).astype(BF16)
    cot = lax.dot_general(pick, cot, over, preferred_element_type=F32).astype(BF16)
    row = lax.broadcasted_iota(jnp.int32, (block, total), 0)
    at = lax.broadcasted_iota(jnp.int32, (block, total), 1)
    fits = at // listed == row
    spread = jnp.where(fits, 1.0, 0.0).astype(BF16)
    cot = jnp.dot(cot, spread, preferred_element_type=F32)
    at = lax.broadcasted_iota(jnp.int32, (8, total), 1)
    to = jnp.full((8, total), -1, jnp.int32)
    for x in range(xs):
        for k in range(listed):
            here = (at // (total // xs) == x) & (at % listed == k)
            to = jnp.where(here, lists[k, x * mids + my_mid], to)
    to = jnp.concatenate([to] * (block // 8), axis=0)
    back = [jnp.where(to[:by_lane] == b, cot, 0.0).astype(BF16) for b in range(blocks)]
    near = got[:, :edges].reshape(total, block)
    back = [jnp.dot(b, near, preferred_element_type=F32) for b in back]
    for mid in range(mids):
        take = jnp.where(fits & (to == my_x * mids + mid), 1.0, 0.0).astype(BF16)
        take = jnp.dot(take, near, preferred_element_type=F32).astype(BF16)
        edges_out[:, mid * block : (mid + 1) * block] = take
    pad = jnp.zeros((-(2 * cols + by_lane) % 16, block), F32)
    parts = []
    for b in range(blocks):
        mine_b = own[:, b * block : (b + 1) * block].astype(F32)
        parts.append(jnp.concatenate([agg[b].astype(F32), mine_b, back[b], pad], axis=0))
    high = parts[0].shape[0]
    parts = [
        jnp.concatenate(parts[x * mids : (x + 1) * mids], axis=0).astype(BF16) for x in range(xs)
    ]
    parts = jnp.concatenate(parts, axis=1)
    row = lax.broadcasted_iota(jnp.int32, (xs * block, block), 0)
    to = lax.broadcasted_iota(jnp.int32, (xs * block, block), 1)
    fits = (to // strip == row // block) & (to % strip == row % strip)
    for low in range(strips):
        move = jnp.where(fits & (row % block // strip == low), 1.0, 0.0).astype(BF16)
        moved = jnp.dot(parts, move, preferred_element_type=F32).astype(BF16)
        for mid in range(mids):
            at = mid * high + 2 * cols
            sends[mid * strips + low, : 2 * cols] = moved[mid * high : at]
            sends[mid * strips + low, 2 * cols + block :] = moved[at : at + by_lane]
    wide = w.shape[2] // lanes
    w = [w[i, :, j * wide : (j + 1) * wide].astype(F32) for i in range(2) for j in range(lanes)]
    w = jnp.concatenate(w, axis=0).astype(BF16)
    for z in range(blocks):
        sends[z, 2 * cols : 2 * cols + block] = w


def sum_nodes(got, sends):
    total = got[0]
    for n in range(1, got.shape[0]):
        total = total + got[n]
    for z in range(sends.shape[0]):
        sends[z] = total.astype(BF16)


def middle(got, w_in, sends, rows, logits, w, sem):
    copy = pltpu.make_async_copy(w_in, w, sem)
    copy.start()
    lanes, wide = got.shape[0], got.shape[2]
    blocks, block, mine = sends.shape[0], got.shape[2], rows.shape[0]
    by_z = (got.shape[1] - 2 * block) // 2 * lanes // blocks
    pre = got[0, : 2 * block].astype(F32)
    for j in range(1, lanes):
        pre = pre + got[j, : 2 * block].astype(F32)
    hidden = jnp.maximum(pre, 0.0).astype(BF16)
    for j in range(lanes):
        rows[:, j * wide : (j + 1) * wide] = hidden[block + j * mine : block + (j + 1) * mine]
    hidden = hidden[:block]
    back = got[:, 2 * block :].astype(F32)
    half = back.shape[1] // 2
    back = (back[:, :half] + back[:, half:]).reshape(lanes * half, block)
    high = back.astype(BF16)
    low = (back - high.astype(F32)).astype(BF16)
    grad = jnp.dot(high, hidden, preferred_element_type=F32)
    grad = grad + jnp.dot(low, hidden, preferred_element_type=F32)
    grad = grad.reshape(blocks, by_z, wide)
    high = grad.astype(BF16)
    sends[:, :by_z] = high
    sends[:, by_z : 2 * by_z] = (grad - high.astype(F32)).astype(BF16)
    over = (((1,), (1,)), ((), ()))
    copy.wait()
    product = lax.dot_general(rows[...], w[0], over, preferred_element_type=F32)
    logits[...] = lax.dot_general(rows[...], w[1], over, preferred_element_type=F32)
    pad = jnp.zeros((mine, 2 * block - product.shape[1]), F32)
    product = jnp.concatenate([product, pad], axis=1)
    rest = product[:, block : block + block // 2]
    rest = jnp.concatenate([rest[: mine // 2], rest[mine // 2 :]], axis=1).astype(BF16)
    product = product[:, :block].astype(BF16)
    for z in range(blocks):
        sends[z, 2 * by_z : 2 * by_z + mine] = product
        sends[z, 2 * by_z + mine :] = rest


def sum_z(got, sends):
    by_z = sends.shape[1]
    total = got[0, : 2 * by_z].astype(F32)
    for z in range(1, got.shape[0]):
        total = total + got[z, : 2 * by_z].astype(F32)
    total = total[:by_z] + total[by_z:]
    for n in range(sends.shape[0]):
        sends[n] = total


def partial_logits(got, near, own_in, sends, own):
    lanes, block = sends.shape[0], sends.shape[2]
    mine = sends.shape[1] // 2
    cores = near.shape[1] // (got.shape[0] * mine)
    above = got.shape[1] - mine - mine // 2
    none = jnp.zeros((mine, block // 2), F32)
    my_c = lax.axis_index("c")
    own[...] = own_in[...]
    rows = []
    for z in range(got.shape[0]):
        rest = got[z, above + mine :].astype(F32)
        rest = jnp.concatenate([rest[:, : block // 2], rest[:, block // 2 :]], axis=0)
        rest = jnp.concatenate([rest, none], axis=1).astype(BF16)
        product = jnp.concatenate([got[z, above : above + mine], rest], axis=1)
        for c in range(cores):
            rows.append(jnp.where(my_c == c, product, jnp.zeros_like(product)))
    rows = jnp.concatenate(rows, axis=0)
    part = jnp.dot(near[...], rows, preferred_element_type=F32).astype(BF16)
    for j in range(lanes):
        sends[j, :mine] = part[j * mine : (j + 1) * mine, :block]
        sends[j, mine:] = part[j * mine : (j + 1) * mine, block:]


def last(grad, logits, sends):
    kept = sends.shape[1] - logits.shape[1]
    by_z = grad.shape[1]
    for j in range(sends.shape[0]):
        for z in range(kept // by_z):
            sends[j, z * by_z : (z + 1) * by_z] = grad[z]
        sends[j, kept:] = logits[j]


def finish(got, own, logits, grad):
    lanes, wide = got.shape[0], got.shape[2]
    mine, cls = logits.shape
    kept = got.shape[1] - 2 * mine
    part = got[0, kept:].astype(F32)
    for j in range(1, lanes):
        part = part + got[j, kept:].astype(F32)
    part = jnp.concatenate([part[:mine], part[mine:]], axis=1)
    logits[...] = part[:, :cls] + own[...]
    for j in range(lanes):
        grad[:, j * wide : (j + 1) * wide] = got[j, :kept].astype(F32)[:cls]


def per_device(features, w_one, adj_one, list_one, adj_two, list_two, w_two, cotangent):
    cols, sources = features.shape
    blocks, fanout = list_one.shape
    block = adj_one.shape[-1]
    mine, listed = adj_two.shape[:2]
    hid, cls = w_two.shape[1:]
    nodes = lax.axis_size("node")
    xs, cores = lax.axis_size("x"), lax.axis_size("c")
    lanes = xs * cores
    wide = hid // lanes
    by_lane = -(-cls // (8 * lanes)) * 8
    every = by_lane * lanes
    by_z = every // blocks
    kept = -(-cls // 8) * 8
    strip = mine * cores
    strips = block // strip
    mids = blocks // xs
    limit = pltpu.CompilerParams(vmem_limit_bytes=16 * 2**20)
    pick_limit = pltpu.CompilerParams(vmem_limit_bytes=64 * 2**20 - 3650 * 2**10)
    wide_limit = pltpu.CompilerParams(vmem_limit_bytes=60 * 2**20)
    away = pl.BlockSpec(memory_space=pltpu.HBM)
    whole = pl.BlockSpec(memory_space=pltpu.VMEM)
    scalars = pl.BlockSpec(memory_space=pltpu.SMEM)
    got = pl.pallas_call(
        near_rows,
        in_specs=[away, away],
        out_shape=jax.ShapeDtypeStruct((lanes, mine * (listed + 2), block), BF16),
        scratch_shapes=[
            pltpu.VMEM((mine * listed, block), BF16),
            pltpu.VMEM((mine, cls), BF16),
            pltpu.SemaphoreType.DMA((2,)),
        ],
        compiler_params=wide_limit,
    )(adj_two.reshape(mine * listed, block), cotangent)
    near = exchange(got, LANE)

    chosen, own = pl.pallas_call(
        pick_blocks,
        in_specs=[scalars, away],
        out_shape=(
            jax.ShapeDtypeStruct((blocks * fanout, cols, block), BF16),
            jax.ShapeDtypeStruct((cols, blocks * block), BF16),
        ),
        scratch_shapes=[pltpu.VMEM((cols, sources), BF16), pltpu.SemaphoreType.DMA],
        compiler_params=pick_limit,
    )(list_one.T, features)
    chosen = chosen.reshape(blocks, fanout, cols, block)
    agg = dot("hkfs,hkts->hft", chosen, adj_one).astype(BF16)
    above = 2 * cols + 2 * cols * lanes
    got, near = pl.pallas_call(
        functools.partial(first, xs, by_lane),
        in_specs=[scalars, whole, whole, whole, whole],
        out_specs=(whole, whole),
        out_shape=(
            jax.ShapeDtypeStruct((blocks, above + by_lane, block), BF16),
            jax.ShapeDtypeStruct((block, mids * block), BF16),
        ),
        compiler_params=limit,
    )(list_two.T, near, agg, own, w_one)
    got = exchange(got, "z")
    inputs, weights, back = jnp.split(got, (2 * cols, above), axis=1)
    inputs = inputs.reshape(blocks, 2, cols, block)
    weights = weights.reshape(blocks, 2, lanes, cols, wide)
    part = dot("zikr,zijkh->jrh", inputs, weights).astype(BF16)
    back = two(jnp.sum(back.astype(F32), axis=0))

    rows = part.reshape(lanes, lanes, mine, wide).transpose(1, 0, 2, 3)
    rows = rows.reshape(lanes, lanes * mine, wide)
    got = exchange(jnp.concatenate([part, rows, to_all(back, lanes)], axis=1), LANE)
    sends, rows, own_logits = pl.pallas_call(
        middle,
        in_specs=[whole, away],
        scratch_shapes=[pltpu.VMEM((2, cls, hid), BF16), pltpu.SemaphoreType.DMA],
        out_shape=(
            jax.ShapeDtypeStruct((blocks, 2 * by_z + mine + mine // 2, block), BF16),
            jax.ShapeDtypeStruct((mine, hid), BF16),
            jax.ShapeDtypeStruct((mine, cls), F32),
        ),
        compiler_params=wide_limit,
    )(got, w_two.transpose(0, 2, 1))
    got = exchange(sends, "z")
    grad = pl.pallas_call(
        sum_z,
        out_shape=jax.ShapeDtypeStruct((nodes, by_z, wide), F32),
        compiler_params=limit,
    )(got)
    grad = pl.pallas_call(
        sum_nodes,
        out_shape=jax.ShapeDtypeStruct((blocks, by_z, wide), BF16),
        compiler_params=limit,
    )(exchange(grad, "node"))

    logits, own_logits = pl.pallas_call(
        partial_logits,
        out_shape=(
            jax.ShapeDtypeStruct((lanes, 2 * mine, block), BF16),
            jax.ShapeDtypeStruct((mine, cls), F32),
        ),
        compiler_params=limit,
    )(got, near, own_logits)

    got = pl.pallas_call(
        last,
        out_shape=jax.ShapeDtypeStruct((lanes, kept + 2 * mine, block), BF16),
        compiler_params=limit,
    )(exchange(grad, "z"), logits)
    got = exchange(got, LANE)
    logits, grad = pl.pallas_call(
        finish,
        out_shape=(
            jax.ShapeDtypeStruct((mine, cls), F32),
            jax.ShapeDtypeStruct((cls, hid), F32),
        ),
        compiler_params=limit,
    )(got, own_logits)
    return rows, logits, grad.T


def solution(mesh):
    nodes = mesh.devices.shape[1]
    fine = Mesh(mesh.devices.reshape(4, 12, 2, nodes), ("x", "z", "c", "node"))
    col = ("x", "z", "c")
    rows = ("node", *col)
    in_specs = (
        P(col, "node"),
        P(None, col, None),
        P("node", None, None, None),
        P("node", None),
        P(rows, None, None),
        P("node", None),
        P(),
        P(rows, None),
    )
    out_specs = (P(rows, None), P(rows, None), P())
    return jax.shard_map(
        per_device, mesh=fine, in_specs=in_specs, out_specs=out_specs, check_vma=False
    )
```

```python
import functools

import jax
import jax.numpy as jnp
from jax import lax
from jax.experimental import pallas as pl
from jax.experimental.pallas import tpu as pltpu
from jax.sharding import Mesh, PartitionSpec as P

F32, BF16 = jnp.float32, jnp.bfloat16
LANE = ("x", "c")


def exchange(parts, axis):
    return lax.all_to_all(parts, axis, 0, 0, tiled=True)


def to_all(part, size):
    return jnp.broadcast_to(part[None], (size, *part.shape))


def dot(spec, a, b):
    return jnp.einsum(spec, a, b, preferred_element_type=F32)


def two(a):
    high = a.astype(BF16)
    return jnp.concatenate([high, (a - high.astype(F32)).astype(BF16)], axis=-2)


def near_rows(edges_in, cot_in, sends, edges, cot, sems):
    copies = [
        pltpu.make_async_copy(edges_in, edges, sems.at[0]),
        pltpu.make_async_copy(cot_in, cot, sems.at[1]),
    ]
    for copy in copies:
        copy.start()
    for copy in copies:
        copy.wait()
    rows, block = edges.shape
    mine, cls = cot.shape
    rest = jnp.concatenate([cot[:, block:], jnp.zeros((mine, 2 * block - cls), BF16)], axis=1)
    for j in range(sends.shape[0]):
        sends[j, :rows] = edges[...]
        sends[j, rows : rows + mine] = cot[:, :block]
        sends[j, rows + mine :] = rest


def pick_blocks(lists, tiles_in, chosen, own, tiles, sem):
    copy = pltpu.make_async_copy(tiles_in, tiles, sem)
    copy.start()
    copy.wait()
    fanout, blocks = lists.shape
    block = chosen.shape[2]
    own[...] = tiles[:, : blocks * block]
    for b in range(blocks):
        for k in range(fanout):
            at = pl.multiple_of(lists[k, b] * block, block)
            chosen[b * fanout + k] = tiles[:, pl.ds(at, block)]


def first(xs, by_lane, lists, got, agg, own, w, sends, edges_out):
    lanes, _, block = got.shape
    blocks, cols = agg.shape[:2]
    listed = lists.shape[0]
    mids = blocks // xs
    strips = blocks // mids
    strip = block // strips
    mine = block // lanes
    my_x, my_mid = lax.axis_index("x"), lax.axis_index("z") // strips
    my_lane = my_x * (lanes // xs) + lax.axis_index("c")
    edges = mine * listed
    total = lanes * edges
    over = (((1,), (1,)), ((), ()))
    cot = [got[:, edges : edges + mine], got[:, edges + mine :]]
    cot = jnp.concatenate([c.reshape(block, block) for c in cot], axis=1)
    shape = (by_lane, 2 * block)
    at = lax.broadcasted_iota(jnp.int32, shape, 1) - lax.broadcasted_iota(jnp.int32, shape, 0)
    pick = jnp.where(at == my_lane * by_lane, 1.0, 0.0).astype(BF16)
    cot = lax.dot_general(pick, cot, over, preferred_element_type=F32).astype(BF16)
    row = lax.broadcasted_iota(jnp.int32, (block, total), 0)
    at = lax.broadcasted_iota(jnp.int32, (block, total), 1)
    fits = at // listed == row
    spread = jnp.where(fits, 1.0, 0.0).astype(BF16)
    cot = jnp.dot(cot, spread, preferred_element_type=F32)
    at = lax.broadcasted_iota(jnp.int32, (8, total), 1)
    to = jnp.full((8, total), -1, jnp.int32)
    for x in range(xs):
        for k in range(listed):
            here = (at // (total // xs) == x) & (at % listed == k)
            to = jnp.where(here, lists[k, x * mids + my_mid], to)
    to = jnp.concatenate([to] * (block // 8), axis=0)
    back = [jnp.where(to[:by_lane] == b, cot, 0.0).astype(BF16) for b in range(blocks)]
    near = got[:, :edges].reshape(total, block)
    back = [jnp.dot(b, near, preferred_element_type=F32) for b in back]
    for mid in range(mids):
        take = jnp.where(fits & (to == my_x * mids + mid), 1.0, 0.0).astype(BF16)
        take = jnp.dot(take, near, preferred_element_type=F32).astype(BF16)
        edges_out[:, mid * block : (mid + 1) * block] = take
    pad = jnp.zeros((-(2 * cols + by_lane) % 16, block), F32)
    parts = []
    for b in range(blocks):
        mine_b = own[:, b * block : (b + 1) * block].astype(F32)
        parts.append(jnp.concatenate([agg[b].astype(F32), mine_b, back[b], pad], axis=0))
    high = parts[0].shape[0]
    parts = [
        jnp.concatenate(parts[x * mids : (x + 1) * mids], axis=0).astype(BF16) for x in range(xs)
    ]
    parts = jnp.concatenate(parts, axis=1)
    row = lax.broadcasted_iota(jnp.int32, (xs * block, block), 0)
    to = lax.broadcasted_iota(jnp.int32, (xs * block, block), 1)
    fits = (to // strip == row // block) & (to % strip == row % strip)
    for low in range(strips):
        move = jnp.where(fits & (row % block // strip == low), 1.0, 0.0).astype(BF16)
        moved = jnp.dot(parts, move, preferred_element_type=F32).astype(BF16)
        for mid in range(mids):
            at = mid * high + 2 * cols
            sends[mid * strips + low, : 2 * cols] = moved[mid * high : at]
            sends[mid * strips + low, 2 * cols + block :] = moved[at : at + by_lane]
    wide = w.shape[2] // lanes
    w = [w[i, :, j * wide : (j + 1) * wide].astype(F32) for i in range(2) for j in range(lanes)]
    w = jnp.concatenate(w, axis=0).astype(BF16)
    for z in range(blocks):
        sends[z, 2 * cols : 2 * cols + block] = w


def sum_nodes(got, sends):
    total = got[0]
    for n in range(1, got.shape[0]):
        total = total + got[n]
    for z in range(sends.shape[0]):
        sends[z] = total.astype(BF16)


def middle(got, w_in, sends, rows, logits, w, sem):
    copy = pltpu.make_async_copy(w_in, w, sem)
    copy.start()
    lanes, wide = got.shape[0], got.shape[2]
    blocks, block, mine = sends.shape[0], got.shape[2], rows.shape[0]
    by_z = (got.shape[1] - 2 * block) // 2 * lanes // blocks
    pre = got[0, : 2 * block].astype(F32)
    for j in range(1, lanes):
        pre = pre + got[j, : 2 * block].astype(F32)
    hidden = jnp.maximum(pre, 0.0).astype(BF16)
    for j in range(lanes):
        rows[:, j * wide : (j + 1) * wide] = hidden[block + j * mine : block + (j + 1) * mine]
    hidden = hidden[:block]
    back = got[:, 2 * block :].astype(F32)
    half = back.shape[1] // 2
    back = (back[:, :half] + back[:, half:]).reshape(lanes * half, block)
    high = back.astype(BF16)
    low = (back - high.astype(F32)).astype(BF16)
    grad = jnp.dot(high, hidden, preferred_element_type=F32)
    grad = grad + jnp.dot(low, hidden, preferred_element_type=F32)
    grad = grad.reshape(blocks, by_z, wide)
    high = grad.astype(BF16)
    sends[:, :by_z] = high
    sends[:, by_z : 2 * by_z] = (grad - high.astype(F32)).astype(BF16)
    over = (((1,), (1,)), ((), ()))
    copy.wait()
    product = lax.dot_general(rows[...], w[0], over, preferred_element_type=F32)
    logits[...] = lax.dot_general(rows[...], w[1], over, preferred_element_type=F32)
    pad = jnp.zeros((mine, 2 * block - product.shape[1]), F32)
    product = jnp.concatenate([product, pad], axis=1)
    rest = product[:, block : block + block // 2]
    rest = jnp.concatenate([rest[: mine // 2], rest[mine // 2 :]], axis=1).astype(BF16)
    product = product[:, :block].astype(BF16)
    for z in range(blocks):
        sends[z, 2 * by_z : 2 * by_z + mine] = product
        sends[z, 2 * by_z + mine :] = rest


def sum_z(got, sends):
    by_z = sends.shape[1]
    total = got[0, : 2 * by_z].astype(F32)
    for z in range(1, got.shape[0]):
        total = total + got[z, : 2 * by_z].astype(F32)
    total = total[:by_z] + total[by_z:]
    for n in range(sends.shape[0]):
        sends[n] = total


def partial_logits(got, near, own_in, sends, own):
    lanes, block = sends.shape[0], sends.shape[2]
    mine = sends.shape[1] // 2
    cores = near.shape[1] // (got.shape[0] * mine)
    above = got.shape[1] - mine - mine // 2
    none = jnp.zeros((mine, block // 2), F32)
    my_c = lax.axis_index("c")
    own[...] = own_in[...]
    rows = []
    for z in range(got.shape[0]):
        rest = got[z, above + mine :].astype(F32)
        rest = jnp.concatenate([rest[:, : block // 2], rest[:, block // 2 :]], axis=0)
        rest = jnp.concatenate([rest, none], axis=1).astype(BF16)
        product = jnp.concatenate([got[z, above : above + mine], rest], axis=1)
        for c in range(cores):
            rows.append(jnp.where(my_c == c, product, jnp.zeros_like(product)))
    rows = jnp.concatenate(rows, axis=0)
    part = jnp.dot(near[...], rows, preferred_element_type=F32).astype(BF16)
    for j in range(lanes):
        sends[j, :mine] = part[j * mine : (j + 1) * mine, :block]
        sends[j, mine:] = part[j * mine : (j + 1) * mine, block:]


def last(grad, logits, sends):
    kept = sends.shape[1] - logits.shape[1]
    by_z = grad.shape[1]
    for j in range(sends.shape[0]):
        for z in range(kept // by_z):
            sends[j, z * by_z : (z + 1) * by_z] = grad[z]
        sends[j, kept:] = logits[j]


def finish(got, own, logits, grad):
    lanes, wide = got.shape[0], got.shape[2]
    mine, cls = logits.shape
    kept = got.shape[1] - 2 * mine
    part = got[0, kept:].astype(F32)
    for j in range(1, lanes):
        part = part + got[j, kept:].astype(F32)
    part = jnp.concatenate([part[:mine], part[mine:]], axis=1)
    logits[...] = part[:, :cls] + own[...]
    for j in range(lanes):
        grad[:, j * wide : (j + 1) * wide] = got[j, :kept].astype(F32)[:cls]


def per_device(features, w_one, adj_one, list_one, adj_two, list_two, w_two, cotangent):
    cols, sources = features.shape
    blocks, fanout = list_one.shape
    block = adj_one.shape[-1]
    mine, listed = adj_two.shape[:2]
    hid, cls = w_two.shape[1:]
    nodes = lax.axis_size("node")
    xs, cores = lax.axis_size("x"), lax.axis_size("c")
    lanes = xs * cores
    wide = hid // lanes
    by_lane = -(-cls // (8 * lanes)) * 8
    every = by_lane * lanes
    by_z = every // blocks
    kept = -(-cls // 8) * 8
    strip = mine * cores
    strips = block // strip
    mids = blocks // xs
    limit = pltpu.CompilerParams(vmem_limit_bytes=16 * 2**20)
    wide_limit = pltpu.CompilerParams(vmem_limit_bytes=60 * 2**20)
    away = pl.BlockSpec(memory_space=pltpu.HBM)
    whole = pl.BlockSpec(memory_space=pltpu.VMEM)
    scalars = pl.BlockSpec(memory_space=pltpu.SMEM)
    got = pl.pallas_call(
        near_rows,
        in_specs=[away, away],
        out_shape=jax.ShapeDtypeStruct((lanes, mine * (listed + 2), block), BF16),
        scratch_shapes=[
            pltpu.VMEM((mine * listed, block), BF16),
            pltpu.VMEM((mine, cls), BF16),
            pltpu.SemaphoreType.DMA((2,)),
        ],
        compiler_params=wide_limit,
    )(adj_two.reshape(mine * listed, block), cotangent)
    near = exchange(got, LANE)

    chosen, own = pl.pallas_call(
        pick_blocks,
        in_specs=[scalars, away],
        out_shape=(
            jax.ShapeDtypeStruct((blocks * fanout, cols, block), BF16),
            jax.ShapeDtypeStruct((cols, blocks * block), BF16),
        ),
        scratch_shapes=[pltpu.VMEM((cols, sources), BF16), pltpu.SemaphoreType.DMA],
        compiler_params=limit,
    )(list_one.T, features)
    chosen = chosen.reshape(blocks, fanout, cols, block)
    agg = dot("hkfs,hkts->hft", chosen, adj_one).astype(BF16)
    above = 2 * cols + 2 * cols * lanes
    got, near = pl.pallas_call(
        functools.partial(first, xs, by_lane),
        in_specs=[scalars, whole, whole, whole, whole],
        out_specs=(whole, whole),
        out_shape=(
            jax.ShapeDtypeStruct((blocks, above + by_lane, block), BF16),
            jax.ShapeDtypeStruct((block, mids * block), BF16),
        ),
        compiler_params=limit,
    )(list_two.T, near, agg, own, w_one)
    got = exchange(got, "z")
    inputs, weights, back = jnp.split(got, (2 * cols, above), axis=1)
    inputs = inputs.reshape(blocks, 2, cols, block)
    weights = weights.reshape(blocks, 2, lanes, cols, wide)
    part = dot("zikr,zijkh->jrh", inputs, weights).astype(BF16)
    back = two(jnp.sum(back.astype(F32), axis=0))

    rows = part.reshape(lanes, lanes, mine, wide).transpose(1, 0, 2, 3)
    rows = rows.reshape(lanes, lanes * mine, wide)
    got = exchange(jnp.concatenate([part, rows, to_all(back, lanes)], axis=1), LANE)
    sends, rows, own_logits = pl.pallas_call(
        middle,
        in_specs=[whole, away],
        scratch_shapes=[pltpu.VMEM((2, cls, hid), BF16), pltpu.SemaphoreType.DMA],
        out_shape=(
            jax.ShapeDtypeStruct((blocks, 2 * by_z + mine + mine // 2, block), BF16),
            jax.ShapeDtypeStruct((mine, hid), BF16),
            jax.ShapeDtypeStruct((mine, cls), F32),
        ),
        compiler_params=wide_limit,
    )(got, w_two.transpose(0, 2, 1))
    got = exchange(sends, "z")
    grad = pl.pallas_call(
        sum_z,
        out_shape=jax.ShapeDtypeStruct((nodes, by_z, wide), F32),
        compiler_params=limit,
    )(got)
    grad = pl.pallas_call(
        sum_nodes,
        out_shape=jax.ShapeDtypeStruct((blocks, by_z, wide), BF16),
        compiler_params=limit,
    )(exchange(grad, "node"))

    logits, own_logits = pl.pallas_call(
        partial_logits,
        out_shape=(
            jax.ShapeDtypeStruct((lanes, 2 * mine, block), BF16),
            jax.ShapeDtypeStruct((mine, cls), F32),
        ),
        compiler_params=limit,
    )(got, near, own_logits)

    got = pl.pallas_call(
        last,
        out_shape=jax.ShapeDtypeStruct((lanes, kept + 2 * mine, block), BF16),
        compiler_params=limit,
    )(exchange(grad, "z"), logits)
    got = exchange(got, LANE)
    logits, grad = pl.pallas_call(
        finish,
        out_shape=(
            jax.ShapeDtypeStruct((mine, cls), F32),
            jax.ShapeDtypeStruct((cls, hid), F32),
        ),
        compiler_params=limit,
    )(got, own_logits)
    return rows, logits, grad.T


def solution(mesh):
    nodes = mesh.devices.shape[1]
    fine = Mesh(mesh.devices.reshape(4, 12, 2, nodes), ("x", "z", "c", "node"))
    col = ("x", "z", "c")
    rows = ("node", *col)
    in_specs = (
        P(col, "node"),
        P(None, col, None),
        P("node", None, None, None),
        P("node", None),
        P(rows, None, None),
        P("node", None),
        P(),
        P(rows, None),
    )
    out_specs = (P(rows, None), P(rows, None), P())
    return jax.shard_map(
        per_device, mesh=fine, in_specs=in_specs, out_specs=out_specs, check_vma=False
    )
```
